256 devices in a mesh: kvp: 64 (over z, x, core), tp: 4 (over y).
Axes of the slice: x: 4, y: 4, z: 8, core: 2. Of those that a mesh axis runs over, the one named last changes fastest.
Arguments:
- query: bfloat16 [64, 16384], P('kvp', 'tp'), may hold values from -24 to 24
- draft_kv: bfloat16 [64, 2, 1024], P('kvp', None, 'tp'), may hold values from -8 to 8
- key_cache: bfloat16 [8, 8192, 1024], P(None, 'kvp', 'tp'), may hold values from -8 to 8
- value_cache: bfloat16 [8, 8192, 1024], P(None, 'kvp', 'tp'), may hold values from -24 to 24
- prompt_of: int32 [32], replicated, may hold values from 0 to 7, as said below
- prefix_len: int32 [8], replicated, may hold values from 2048 to 8192, as said below
- out_weight: bfloat16 [16384, 16384], P('tp', 'kvp'), may hold values from -1 to 1
- stream: bfloat16 [64, 16384], P('tp', 'kvp'), may hold values from -6 to 6
- norm_gain: bfloat16 [16384], P('kvp'), may hold values from 0.099609375 to 1.8984375
- gate_up: bfloat16 [2, 26624, 16384], P(None, ('kvp', 'tp')), may hold values from -0.046875 to 0.046875
- down_weight: bfloat16 [26624, 16384], P(('kvp', 'tp')), may hold values from -0.0390625 to 0.0390625
Outputs:
- layer_out: bfloat16 [64, 16384], P('tp', 'kvp')
The draws below stay inside these ranges and needn't reach their ends.
Inputs may be any that keep to these rules, and one draw needn't show every extreme that they name: `prompt_of`: each prompt id appears for exactly 4 samples. `prefix_len`: some prompt has the full length 8192.
All inputs are finite; a program needn't handle non-finite values.
Results may differ from the reference program's by a relative error of at most 0.01.
Values may be sent and summed in bfloat16 or wider, within the bound.
No kernel may reach another device: no remote copies, remote signals or barrier semaphores. Data moves between devices by JAX's collectives and lax.ppermute only.
A program may use at most 128 MiB of HBM per device.

```python
import jax
import jax.numpy as jnp
from jax import lax

D = 16384
H = 128
KVH = 8
HD = 128
FFW = 26624
PROMPTS = 8
ROWS = 32
TOKS = 64
CTX = 8192


def sink_signs(key):
    bits = jax.random.randint(jax.random.fold_in(key, 101), (KVH, HD), 0, 2)
    return (2 * bits - 1).astype(jnp.float32)


def offset_signs(key):
    bits = jax.random.randint(jax.random.fold_in(key, 103), (KVH * HD,), 0, 2)
    return (2 * bits - 1).astype(jnp.float32)


def sink_rows(key):
    start = jax.random.randint(jax.random.fold_in(key, 107), (PROMPTS,), 0, CTX // 4 - 1).astype(jnp.int32)
    position = jnp.arange(CTX, dtype=jnp.int32)
    first = (position[None, :] == start[:, None])[:, :, None]
    second = (position[None, :] == start[:, None] + 1)[:, :, None]
    return (first, second)


def draw_query(key, part):
    signs = sink_signs(key)
    key = jax.random.fold_in(key, 5)
    key_noise = jax.random.fold_in(key, 0)
    key_mask = jax.random.fold_in(key, 2)
    key_pull = jax.random.fold_in(key, 3)
    jitter = jax.random.normal(key_noise, (TOKS, H, HD), jnp.float32)
    planted = jax.random.randint(key_mask, (TOKS, H), 0, 8) == 0
    pull = jax.random.uniform(key_pull, (TOKS, H), jnp.float32, 1.5, 3.5) * (16.0 * HD ** (-0.5))
    head_signs = jnp.repeat(signs, H // KVH, axis=0)
    sink_part = jnp.where(planted, pull, 0.0)[:, :, None] * head_signs[None, :, :]
    result = jitter + sink_part
    return jnp.clip(result, -24.0, 24.0).reshape(TOKS, H * HD).astype(jnp.bfloat16)


def draw_draft_kv(key, part):
    offset = 0.5 * offset_signs(key)
    key = jax.random.fold_in(key, 7)
    key_noise, key_value = jax.random.split(key)
    draft_keys = jax.random.normal(key_noise, (TOKS, KVH, HD), jnp.float32)
    values = jax.random.normal(key_value, (TOKS, KVH * HD), jnp.float32)
    draft_keys = 2.5 * draft_keys
    values = 3.5 * values + offset[None, :]
    stacked = jnp.stack([draft_keys.reshape(TOKS, KVH * HD), values], 1)
    return jnp.clip(stacked, -8.0, 8.0).astype(jnp.bfloat16)


def draw_key_cache(key, part):
    signs = sink_signs(key).reshape(KVH * HD)
    first, second = sink_rows(key)
    key = jax.random.fold_in(key, 15)
    base = jnp.clip(2.0 * jax.random.normal(key, (PROMPTS, CTX, KVH * HD), jnp.float32), -8.0, 8.0)
    result = jnp.where(first, 8.0 * signs[None, None, :], jnp.where(second, 7.9375 * signs[None, None, :], base))
    return result.astype(jnp.bfloat16)


def draw_value_cache(key, part):
    offset = 0.5 * offset_signs(key)
    first, second = sink_rows(key)
    key = jax.random.fold_in(key, 17)
    key_base, key_sink = jax.random.split(key)
    base = 4.0 * jax.random.normal(key_base, (PROMPTS, CTX, KVH * HD), jnp.float32)
    small = 0.5 * jax.random.normal(key_sink, (PROMPTS, CTX, KVH * HD), jnp.float32)
    result = jnp.where(first | second, small, base) + offset[None, None, :]
    return jnp.clip(result, -24.0, 24.0).astype(jnp.bfloat16)


def draw_out_weight(key, part):
    offset = offset_signs(key)
    spread = jnp.repeat(offset.reshape(KVH, HD), H // KVH, axis=0).reshape(H * HD)
    key = jax.random.fold_in(key, 19)
    key_base, key_col = jax.random.split(key)
    column = (2 * jax.random.randint(key_col, (D,), 0, 2) - 1).astype(jnp.float32)
    base = jnp.clip(jax.random.normal(key_base, (H * HD, D), jnp.float32), -6.0, 6.0)
    pull = 3.0
    result = base * (H * HD) ** (-0.5) + pull / (H * HD) * spread[:, None] * column[None, :]
    return result.astype(jnp.bfloat16)


def draw_prompt_of(key, part):
    key = jax.random.fold_in(key, 9)
    return (jax.random.permutation(key, ROWS) % PROMPTS).astype(jnp.int32)


def draw_prefix_len(key, part):
    key = jax.random.fold_in(key, 11)
    key_len, key_full = jax.random.split(key)
    lengths = jax.random.randint(key_len, (PROMPTS,), CTX // 4, CTX + 1).astype(jnp.int32)
    longest = jax.random.randint(key_full, (), 0, PROMPTS).astype(jnp.int32)
    return jnp.where(jnp.arange(PROMPTS, dtype=jnp.int32) == longest, CTX, lengths).astype(jnp.int32)


def draw_stream(key, part):
    key = jax.random.fold_in(key, 13)
    position = jnp.arange(D, dtype=jnp.float32) / D
    base = jax.random.normal(key, (TOKS, D), jnp.float32)
    result = base * (0.3 * jnp.exp(position * 1.1))[None, :]
    return jnp.clip(result, -6.0, 6.0).astype(jnp.bfloat16)


def level_of(key, shape, cuts, low, largest):
    level, own = 1.0, jax.random.fold_in(key, 6)
    for dim, parts in cuts:
        steps = jnp.exp(jax.random.uniform(jax.random.fold_in(own, dim), (parts,), jnp.float32, low / len(cuts), largest / len(cuts)))
        level = level * jnp.repeat(steps, shape[dim] // parts).reshape([-1 if axis == dim else 1 for axis in range(len(shape))])
    return level


def noise(own_key, dims, scale, reach, shards=(), kind=jnp.bfloat16):
    entries = scale * jax.random.normal(own_key, dims, jnp.float32)
    if shards:
        entries = entries * level_of(own_key, dims, shards, -0.22, 0.18)
    return jnp.clip(entries, -reach, reach).astype(kind)


def setup_inputs(seed: int = 0) -> dict:
    key_list = jax.random.split(jax.random.key(seed), 12)
    query = draw_query(jax.random.fold_in(key_list[11], 71), 0)
    draft_kv = draw_draft_kv(jax.random.fold_in(key_list[11], 71), 0)
    key_cache = draw_key_cache(jax.random.fold_in(key_list[11], 71), 0)
    value_cache = draw_value_cache(jax.random.fold_in(key_list[11], 71), 0)
    prompt_of = draw_prompt_of(jax.random.fold_in(key_list[11], 71), 0)
    prefix_len = draw_prefix_len(jax.random.fold_in(key_list[11], 71), 0)
    out_weight = draw_out_weight(jax.random.fold_in(key_list[11], 71), 0)
    stream = draw_stream(jax.random.fold_in(key_list[11], 71), 0)
    norm_gain = jnp.clip(1.0 + 0.18 * jax.random.normal(key_list[8], (D,), jnp.float32), 0.099609375, 1.8984375).astype(jnp.bfloat16)
    gate_up = noise(key_list[9], (2, FFW, D), D ** -0.5, 0.046875, ((1, 256),))
    down_weight = noise(key_list[10], (FFW, D), FFW ** -0.5, 0.0390625, ((0, 256),))
    return dict(query=query, draft_kv=draft_kv, key_cache=key_cache, value_cache=value_cache, prompt_of=prompt_of, prefix_len=prefix_len, out_weight=out_weight, stream=stream, norm_gain=norm_gain, gate_up=gate_up, down_weight=down_weight)


floor_score = -1e+30

def reference(query, draft_kv, key_cache, value_cache, prompt_of, prefix_len, out_weight, stream, norm_gain, gate_up, down_weight):
    groups = H // KVH
    score_scale = HD ** (-0.5)
    queries = query.reshape(TOKS, KVH, groups, HD)
    draft_keys = draft_kv[:, 0].reshape(TOKS, KVH, HD).astype(jnp.float32)
    draft_values = draft_kv[:, 1].reshape(TOKS, KVH, HD).astype(jnp.float32)
    token_ids = jnp.arange(TOKS, dtype=jnp.int32)
    token_row = token_ids % ROWS
    token_step = token_ids // ROWS
    token_prompt = prompt_of[token_row]
    token_len = prefix_len[token_prompt]

    def per_token(index):
        current = queries[index].astype(jnp.float32)
        prompt = token_prompt[index]
        cache_keys = key_cache[prompt].reshape(CTX, KVH, HD).astype(jnp.float32)
        cache_values = value_cache[prompt].reshape(CTX, KVH, HD).astype(jnp.float32)
        scores = jnp.einsum('kgd,ckd->kgc', current, cache_keys) * score_scale
        visible = jnp.arange(CTX, dtype=jnp.int32) < token_len[index]
        own_draft = (token_row == token_row[index]) & (token_step <= token_step[index])
        draft_scores = jnp.einsum('kgd,ukd->kgu', current, draft_keys) * score_scale
        local_max = jnp.maximum(lax.optimization_barrier(jnp.max(jnp.where(visible, scores, floor_score), -1)), lax.optimization_barrier(jnp.max(jnp.where(own_draft, draft_scores, floor_score), -1)))
        shifted = jnp.where(visible, jnp.exp(scores - local_max[..., None]), 0.0)
        draft_weights = jnp.where(own_draft, jnp.exp(draft_scores - local_max[..., None]), 0.0)
        totals = lax.optimization_barrier(jnp.sum(shifted, -1)) + lax.optimization_barrier(jnp.sum(draft_weights, -1))
        weighted = jnp.einsum('kgc,ckd->kgd', shifted.astype(jnp.bfloat16).astype(jnp.float32), cache_values)
        weighted = weighted + jnp.einsum('kgu,ukd->kgd', draft_weights.astype(jnp.bfloat16).astype(jnp.float32), draft_values)
        return (weighted / totals[..., None]).reshape(H * HD)
    attn = lax.map(per_token, token_ids).astype(jnp.bfloat16)
    middle = stream.astype(jnp.float32) + jnp.dot(attn, out_weight, preferred_element_type=jnp.float32)
    square_mean = lax.optimization_barrier(jnp.sum(middle * middle, 1)) / D
    normed = (middle * lax.rsqrt(square_mean + 1e-05)[:, None] * norm_gain.astype(jnp.float32)).astype(jnp.bfloat16)
    gate_value = jnp.dot(normed, gate_up[0].T, preferred_element_type=jnp.float32)
    up_value = jnp.dot(normed, gate_up[1].T, preferred_element_type=jnp.float32)
    hidden = (jax.nn.silu(gate_value) * up_value).astype(jnp.bfloat16)
    return (middle + jnp.dot(hidden, down_weight, preferred_element_type=jnp.float32)).astype(jnp.bfloat16)
```

```python
import jax
import jax.numpy as jnp
from jax import lax
from jax.experimental import pallas as pl
from jax.experimental.pallas import tpu as pltpu
from jax.sharding import PartitionSpec as P

D = 16384
HD = 128
NZ, NX, NC, NY = 8, 4, 2, 4
PEERS = NZ * NX
HEADS = 32
GROUP = 16
PROMPTS = 8
TOKS = 64
HALF = 32
SHARD = 128
COLS = 256
EPS = 1e-05
SCALE = HD ** (-0.5)
FLOOR = -1e30
VMEM_LIMIT = 56 * 1024 * 1024

bf16 = jnp.bfloat16
f32 = jnp.float32


def kvp_index(z, x, c):
    return (z * NX + x) * NC + c


def all_index(z, x, c, y):
    return kvp_index(z, x, c) * NY + y


G_XZ = [[kvp_index(z, x, c) for z in range(NZ) for x in range(NX)] for c in range(NC)]
G_Z = [[kvp_index(z, x, c) for z in range(NZ)] for x in range(NX) for c in range(NC)]
G_XY = [
    [all_index(z, x, c, y) for x in range(NX) for y in range(NY)]
    for z in range(NZ)
    for c in range(NC)
]
CORE_PAIRS = [(i, i ^ 1) for i in range(NZ * NX * NC)]


def swap_cores(array):
    return lax.ppermute(array, "kvp", CORE_PAIRS)


def swap_plane(array):
    return lax.all_to_all(array, "kvp", 0, 0, axis_index_groups=G_XZ, tiled=True)


def nt_dot(a, b):
    return lax.dot_general(a, b, (((1,), (1,)), ((), ())), preferred_element_type=f32)


def nn_dot(a, b):
    return jnp.dot(a, b, preferred_element_type=f32)


def lane_ids(shape):
    return lax.broadcasted_iota(jnp.int32, shape, len(shape) - 1)


def row_ids(shape):
    return lax.broadcasted_iota(jnp.int32, shape, len(shape) - 2)


def stats_tile(rows, top, total):
    lanes = lane_ids((rows, HD))
    high = total.astype(bf16).astype(f32)
    low = total - high
    return jnp.where(
        lanes == 0, top, jnp.where(lanes == 1, high, jnp.where(lanes == 2, low, 0.0))
    )


def attention_kernel(
    prompt_ref, len_ref, own_ref, oth_ref, k_ref, v_ref, keep_ref, send_ref, order_ref, gath, count
):
    kvp = lax.axis_index("kvp")
    core = lax.rem(kvp, 2)
    for p in range(PROMPTS):
        count[p] = 0
    for s in range(HALF):
        p = prompt_ref[s]
        seen = jnp.minimum(count[p], 3)
        count[p] = seen + 1
        order_ref[p * 8 + seen] = s
        order_ref[p * 8 + 4 + seen] = s + HALF
    gath[0:PEERS] = own_ref[...]
    gath[PEERS : 2 * PEERS] = oth_ref[...]
    to_row = row_ids((256, 256))
    from_row = lane_ids((256, 256))
    regroup = (
        (to_row // GROUP == from_row % GROUP) & (to_row % GROUP == from_row // GROUP)
    ).astype(bf16)
    position = kvp * SHARD + lane_ids((SHARD, SHARD))
    for pair in range(4):
        out_ref = keep_ref if pair < 2 else send_ref
        for kv in range(2):
            parts = []
            for q_ in range(2):
                p = lax.rem(pair * 2 + q_ + 4 * core, PROMPTS)
                tiles = []
                for j in range(8):
                    t = order_ref[p * 8 + j]
                    row = t // 2 + PEERS * lax.rem(t + core, 2)
                    tiles.append(gath[row, kv * GROUP : (kv + 1) * GROUP, :])
                queries = jnp.concatenate(tiles, axis=0)
                keys = k_ref[p, :, kv * HD : (kv + 1) * HD]
                values = v_ref[p, :, kv * HD : (kv + 1) * HD]
                scores = nt_dot(queries, keys) * SCALE
                visible = position < len_ref[p]
                top = jnp.max(jnp.where(visible, scores, FLOOR), axis=1, keepdims=True)
                top = top.astype(bf16).astype(f32)
                weights = jnp.where(visible, jnp.exp(scores - top), 0.0)
                total = jnp.sum(weights, axis=1, keepdims=True)
                summed = nn_dot(weights.astype(bf16), values)
                parts.append(
                    jnp.concatenate(
                        [summed.astype(bf16), stats_tile(SHARD, top, total).astype(bf16)], axis=1
                    )
                )
            both = nn_dot(regroup, jnp.concatenate(parts, axis=0)).astype(bf16)
            first = (pair % 2) * 16
            for g in range(GROUP):
                out_ref[kv * GROUP + g, first : first + 16, :] = both[g * 16 : (g + 1) * 16, :]


def merge_kernel(a_ref, b_ref, out_ref):
    def step(h, carry):
        a = a_ref[h].astype(f32)
        b = b_ref[h].astype(f32)
        top_a, top_b = a[:, HD : HD + 1], b[:, HD : HD + 1]
        top = jnp.maximum(top_a, top_b)
        fa, fb = jnp.exp(top_a - top), jnp.exp(top_b - top)
        total = fa * (a[:, HD + 1 : HD + 2] + a[:, HD + 2 : HD + 3]) + fb * (
            b[:, HD + 1 : HD + 2] + b[:, HD + 2 : HD + 3]
        )
        out_ref[h, :, :HD] = (fa * a[:, :HD] + fb * b[:, :HD]).astype(bf16)
        out_ref[h, :, HD:] = stats_tile(HALF, top, total).astype(bf16)
        return carry

    lax.fori_loop(0, HEADS, step, 0, unroll=True)


def combine_kernel(order_ref, part_ref, own_ref, oth_ref, out_ref, gath):
    kvp = lax.axis_index("kvp")
    core = lax.rem(kvp, 2)
    head = kvp // 2
    kv = head // GROUP
    gath[0:PEERS] = own_ref[...]
    gath[PEERS : 2 * PEERS] = oth_ref[...]
    first = pl.multiple_of(kv * GROUP, GROUP)
    query_tiles, draft_tiles = [], []
    for s in range(HALF):
        t = order_ref[HALF * core + s]
        row = t // 2 + PEERS * lax.rem(t + core, 2)
        query_tiles.append(gath[row, pl.ds(first, GROUP), :])
        draft_tiles.append(gath[row, HEADS : HEADS + GROUP, :])
    shape = (HALF, HALF * GROUP)
    slot = row_ids(shape)
    other = lane_ids(shape) // GROUP
    inner = lane_ids(shape) % GROUP
    pick = ((slot == other) & (inner == head % GROUP)).astype(bf16)
    queries = nn_dot(pick, jnp.concatenate(query_tiles, axis=0)).astype(bf16)
    drafts = jnp.concatenate(draft_tiles, axis=0)
    scores = nt_dot(queries, drafts) * SCALE
    visible = (
        (slot // 8 == other // 8)
        & (slot % 4 == other % 4)
        & ((other // 4) % 2 <= (slot // 4) % 2)
        & (inner == kv)
    )
    top = jnp.max(jnp.where(visible, scores, FLOOR), axis=1, keepdims=True)
    for i in range(PEERS):
        top = jnp.maximum(top, part_ref[i, :, HD : HD + 1].astype(f32))
    weights = jnp.where(visible, jnp.exp(scores - top), 0.0)
    total = jnp.sum(weights, axis=1, keepdims=True)
    summed = nn_dot(pltpu.roll(weights, 2, 1).astype(bf16), drafts)
    for i in range(PEERS):
        part = part_ref[i].astype(f32)
        factor = jnp.exp(part[:, HD : HD + 1] - top)
        total = total + factor * (part[:, HD + 1 : HD + 2] + part[:, HD + 2 : HD + 3])
        summed = summed + factor * part[:, :HD]
    attn = (summed / total).astype(bf16)
    for i in range(PEERS):
        out_ref[i] = attn


def project_kernel(order_ref, own_ref, oth_ref, w_ref, stream_ref, out_ref, by_slot, by_token):
    kvp = lax.axis_index("kvp")
    core = lax.rem(kvp, 2)
    tp = lax.axis_index("tp")
    acc = jnp.zeros((TOKS, COLS), f32)
    for i in range(HEADS // 2):
        lhs = jnp.concatenate(
            [
                jnp.concatenate([own_ref[2 * i], own_ref[2 * i + 1]], axis=1),
                jnp.concatenate([oth_ref[2 * i], oth_ref[2 * i + 1]], axis=1),
            ],
            axis=0,
        )
        acc = acc + nn_dot(lhs, w_ref[2 * i * HD : (2 * i + 2) * HD, :])
    by_slot[...] = acc
    for r in range(TOKS):
        t = order_ref[lax.rem(r + HALF * core, TOKS)]
        by_token[pl.ds(t, 1), :] = by_slot[r : r + 1, :]
    mine = pl.ds(pl.multiple_of(tp * 16, 16), 16)
    by_token[mine, :] = by_token[mine, :] + stream_ref[...].astype(f32)
    for i in range(NY):
        out_ref[i] = by_token[...]


def norm_kernel(parts_ref, gain_ref, msg_ref, mid_ref, whole):
    tp = lax.axis_index("tp")
    middle = (parts_ref[0] + parts_ref[1]) + (parts_ref[2] + parts_ref[3])
    whole[...] = middle
    mid_ref[...] = whole[pl.ds(pl.multiple_of(tp * 16, 16), 16), :]
    scaled = (middle * gain_ref[...].astype(f32)).astype(bf16)
    squares = jnp.sum(middle * middle, axis=1, keepdims=True)
    high = squares.astype(bf16).astype(f32)
    low = squares - high
    lanes = lane_ids((16, HD))
    stats = jnp.zeros((16, HD), f32)
    for j in range(4):
        stats = jnp.where(lanes == 2 * j, high[16 * j : 16 * j + 16], stats)
        stats = jnp.where(lanes == 2 * j + 1, low[16 * j : 16 * j + 16], stats)
    block = jnp.concatenate(
        [scaled[16 * j : 16 * j + 16] for j in range(4)] + [stats.astype(bf16)], axis=1
    )
    for i in range(PEERS):
        msg_ref[i] = block


def feed_kernel(own_ref, oth_ref, gu_ref, down_ref, send_ref, keep_ref):
    core = lax.rem(lax.axis_index("kvp"), 2)
    gate = jnp.zeros((TOKS, 104), f32)
    up = jnp.zeros((TOKS, 104), f32)
    stats = jnp.zeros((16, HD), f32)
    for i in range(PEERS):
        for src_ref, side in ((own_ref, core), (oth_ref, 1 - core)):
            rows = jnp.concatenate(
                [src_ref[i, :, COLS * j : COLS * (j + 1)] for j in range(4)], axis=0
            )
            cols = pl.ds(pl.multiple_of((2 * i + side) * COLS, COLS), COLS)
            gate = gate + nt_dot(rows, gu_ref[0, :, cols])
            up = up + nt_dot(rows, gu_ref[1, :, cols])
            stats = stats + src_ref[i, :, 4 * COLS :].astype(f32)
    squares = jnp.concatenate(
        [stats[:, 2 * j : 2 * j + 1] + stats[:, 2 * j + 1 : 2 * j + 2] for j in range(4)], axis=0
    )
    rscale = lax.rsqrt(squares / D + EPS)
    gate = gate * rscale
    up = up * rscale
    hidden = (gate / (1.0 + jnp.exp(-gate)) * up).astype(bf16)
    for out_ref, side in ((send_ref, 1 - core), (keep_ref, core)):
        for z in range(NZ):
            for x in range(NX):
                cols = pl.ds(pl.multiple_of((2 * (z * NX + x) + side) * COLS, COLS), COLS)
                part = nn_dot(hidden, down_ref[:, cols]).astype(out_ref.dtype)
                for y in range(NY):
                    out_ref[x * NY + y, z * 16 : (z + 1) * 16, :] = part[16 * y : 16 * y + 16]


VMEM = pl.BlockSpec(memory_space=pltpu.VMEM)
SMEM = pl.BlockSpec(memory_space=pltpu.SMEM)
PARAMS = pltpu.CompilerParams(vmem_limit_bytes=VMEM_LIMIT)


def call(kernel, name, in_specs, out_shape, out_specs, scratch=()):
    return pl.pallas_call(
        kernel,
        name=name,
        in_specs=in_specs,
        out_shape=out_shape,
        out_specs=out_specs,
        scratch_shapes=list(scratch),
        compiler_params=PARAMS,
    )


def on_device(
    query,
    draft_kv,
    key_cache,
    value_cache,
    prompt_of,
    prefix_len,
    out_weight,
    stream,
    norm_gain,
    gate_up,
    down_weight,
):
    shape = jax.ShapeDtypeStruct
    block = jnp.concatenate(
        [query.reshape(HEADS, HD), draft_kv.reshape(4, HD), jnp.zeros((12, HD), bf16)], axis=0
    )
    own = swap_plane(jnp.broadcast_to(block[None], (PEERS, 48, HD)))
    oth = swap_cores(own)
    keep, send, order = call(
        attention_kernel,
        "attention",
        [SMEM, SMEM, VMEM, VMEM, VMEM, VMEM],
        [
            shape((HEADS, HALF, 2 * HD), bf16),
            shape((HEADS, HALF, 2 * HD), bf16),
            shape((TOKS,), jnp.int32),
        ],
        [VMEM, VMEM, SMEM],
        [pltpu.VMEM((2 * PEERS, 48, HD), bf16), pltpu.SMEM((PROMPTS,), jnp.int32)],
    )(prompt_of, prefix_len, own, oth, key_cache, value_cache)
    merged = call(
        merge_kernel, "merge", [VMEM, VMEM], shape((HEADS, HALF, 2 * HD), bf16), VMEM
    )(keep, swap_cores(send))
    attn = call(
        combine_kernel,
        "combine",
        [SMEM, VMEM, VMEM, VMEM],
        shape((PEERS, HALF, HD), bf16),
        VMEM,
        [pltpu.VMEM((2 * PEERS, 48, HD), bf16)],
    )(order, swap_plane(merged), own, oth)
    attn_own = swap_plane(attn)
    attn_oth = swap_cores(attn_own)
    partial = call(
        project_kernel,
        "project",
        [SMEM, VMEM, VMEM, VMEM, VMEM],
        shape((NY, TOKS, COLS), f32),
        VMEM,
        [pltpu.VMEM((TOKS, COLS), f32), pltpu.VMEM((TOKS, COLS), f32)],
    )(order, attn_own, attn_oth, out_weight, stream)
    partial = lax.all_to_all(partial, "tp", 0, 0, tiled=True)
    msg, middle = call(
        norm_kernel,
        "norm",
        [VMEM, VMEM],
        [shape((PEERS, 16, 4 * COLS + HD), bf16), shape((16, COLS), f32)],
        [VMEM, VMEM],
        [pltpu.VMEM((TOKS, COLS), f32)],
    )(partial, norm_gain.reshape(1, COLS))
    normed_own = swap_plane(msg)
    normed_oth = swap_cores(normed_own)
    send, keep = call(
        feed_kernel,
        "feed",
        [VMEM, VMEM, VMEM, VMEM],
        [shape((NX * NY, NZ * 16, COLS), bf16), shape((NX * NY, NZ * 16, COLS), f32)],
        [VMEM, VMEM],
    )(normed_own, normed_oth, gate_up, down_weight)
    summed = (keep + swap_cores(send).astype(f32)).astype(bf16)
    summed = lax.all_to_all(summed, ("kvp", "tp"), 0, 0, axis_index_groups=G_XY, tiled=True)
    summed = jnp.sum(summed.astype(f32), axis=0).astype(bf16).reshape(NZ, 16, COLS)
    summed = lax.all_to_all(summed, "kvp", 0, 0, axis_index_groups=G_Z, tiled=True)
    return (middle + jnp.sum(summed.astype(f32), axis=0)).astype(bf16)


def solution(mesh):
    in_specs = (
        P("kvp", "tp"),
        P("kvp", None, "tp"),
        P(None, "kvp", "tp"),
        P(None, "kvp", "tp"),
        P(),
        P(),
        P("tp", "kvp"),
        P("tp", "kvp"),
        P("kvp"),
        P(None, ("kvp", "tp"), None),
        P(("kvp", "tp"), None),
    )
    out_specs = P("tp", "kvp")
    return jax.shard_map(
        on_device, mesh=mesh, in_specs=in_specs, out_specs=out_specs, check_vma=False
    )
```

```python
import jax
import jax.numpy as jnp
from jax import lax
from jax.experimental import pallas as pl
from jax.experimental.pallas import tpu as pltpu
from jax.sharding import PartitionSpec as P

D = 16384
HD = 128
NZ, NX, NC, NY = 8, 4, 2, 4
PEERS = NZ * NX
HEADS = 32
GROUP = 16
PROMPTS = 8
TOKS = 64
HALF = 32
SHARD = 128
COLS = 256
EPS = 1e-05
SCALE = HD ** (-0.5)
FLOOR = -1e30
VMEM_LIMIT = 24 * 1024 * 1024

bf16 = jnp.bfloat16
f32 = jnp.float32


def kvp_index(z, x, c):
    return (z * NX + x) * NC + c


def all_index(z, x, c, y):
    return kvp_index(z, x, c) * NY + y


G_XZ = [[kvp_index(z, x, c) for z in range(NZ) for x in range(NX)] for c in range(NC)]
G_Z = [[kvp_index(z, x, c) for z in range(NZ)] for x in range(NX) for c in range(NC)]
G_XY = [
    [all_index(z, x, c, y) for x in range(NX) for y in range(NY)]
    for z in range(NZ)
    for c in range(NC)
]
CORE_PAIRS = [(i, i ^ 1) for i in range(NZ * NX * NC)]


def swap_cores(array):
    return lax.ppermute(array, "kvp", CORE_PAIRS)


def swap_plane(array):
    return lax.all_to_all(array, "kvp", 0, 0, axis_index_groups=G_XZ, tiled=True)


def nt_dot(a, b):
    return lax.dot_general(a, b, (((1,), (1,)), ((), ())), preferred_element_type=f32)


def nn_dot(a, b):
    return jnp.dot(a, b, preferred_element_type=f32)


def lane_ids(shape):
    return lax.broadcasted_iota(jnp.int32, shape, len(shape) - 1)


def row_ids(shape):
    return lax.broadcasted_iota(jnp.int32, shape, len(shape) - 2)


def stats_tile(rows, top, total):
    lanes = lane_ids((rows, HD))
    high = total.astype(bf16).astype(f32)
    low = total - high
    return jnp.where(
        lanes == 0, top, jnp.where(lanes == 1, high, jnp.where(lanes == 2, low, 0.0))
    )


def attention_kernel(
    prompt_ref, len_ref, own_ref, oth_ref, k_ref, v_ref, k2_ref, v2_ref, out_ref, order_ref, gath, count
):
    kvp = lax.axis_index("kvp")
    core = lax.rem(kvp, 2)
    for p in range(PROMPTS):
        count[p] = 0
    for s in range(HALF):
        p = prompt_ref[s]
        seen = jnp.minimum(count[p], 3)
        count[p] = seen + 1
        order_ref[p * 8 + seen] = s
        order_ref[p * 8 + 4 + seen] = s + HALF
    gath[0:PEERS] = own_ref[...]
    gath[PEERS : 2 * PEERS] = oth_ref[...]
    to_row = row_ids((256, 256))
    from_row = lane_ids((256, 256))
    regroup = (
        (to_row // GROUP == from_row % GROUP) & (to_row % GROUP == from_row // GROUP)
    ).astype(bf16)
    here = kvp * SHARD + lane_ids((SHARD, SHARD))
    there = (kvp + 1 - 2 * core) * SHARD + lane_ids((SHARD, SHARD))
    position = jnp.concatenate([here, there], axis=1)
    for pair in range(2):
        for kv in range(2):
            cols = slice(kv * HD, (kv + 1) * HD)
            parts = []
            for q_ in range(2):
                p = pair * 2 + q_ + 4 * core
                tiles = []
                for j in range(8):
                    t = order_ref[p * 8 + j]
                    row = t // 2 + PEERS * lax.rem(t + core, 2)
                    tiles.append(gath[row, kv * GROUP : (kv + 1) * GROUP, :])
                queries = jnp.concatenate(tiles, axis=0)
                keys = jnp.concatenate([k_ref[p, :, cols], k2_ref[p, :, cols]], axis=0)
                values = jnp.concatenate([v_ref[p, :, cols], v2_ref[p, :, cols]], axis=0)
                scores = nt_dot(queries, keys) * SCALE
                visible = position < len_ref[p]
                top = jnp.max(jnp.where(visible, scores, FLOOR), axis=1, keepdims=True)
                top = top.astype(bf16).astype(f32)
                weights = jnp.where(visible, jnp.exp(scores - top), 0.0)
                total = jnp.sum(weights, axis=1, keepdims=True)
                summed = nn_dot(weights.astype(bf16), values)
                parts.append(
                    jnp.concatenate(
                        [summed.astype(bf16), stats_tile(SHARD, top, total).astype(bf16)], axis=1
                    )
                )
            both = nn_dot(regroup, jnp.concatenate(parts, axis=0)).astype(bf16)
            for g in range(GROUP):
                out_ref[kv * GROUP + g, pair * 16 : pair * 16 + 16, :] = both[
                    g * 16 : (g + 1) * 16, :
                ]


def combine_kernel(order_ref, part_ref, own_ref, oth_ref, out_ref, gath):
    kvp = lax.axis_index("kvp")
    core = lax.rem(kvp, 2)
    head = kvp // 2
    kv = head // GROUP
    gath[0:PEERS] = own_ref[...]
    gath[PEERS : 2 * PEERS] = oth_ref[...]
    first = pl.multiple_of(kv * GROUP, GROUP)
    query_tiles, draft_tiles = [], []
    for s in range(HALF):
        t = order_ref[HALF * core + s]
        row = t // 2 + PEERS * lax.rem(t + core, 2)
        query_tiles.append(gath[row, pl.ds(first, GROUP), :])
        draft_tiles.append(gath[row, HEADS : HEADS + GROUP, :])
    shape = (HALF, HALF * GROUP)
    slot = row_ids(shape)
    other = lane_ids(shape) // GROUP
    inner = lane_ids(shape) % GROUP
    pick = ((slot == other) & (inner == head % GROUP)).astype(bf16)
    queries = nn_dot(pick, jnp.concatenate(query_tiles, axis=0)).astype(bf16)
    drafts = jnp.concatenate(draft_tiles, axis=0)
    scores = nt_dot(queries, drafts) * SCALE
    visible = (
        (slot // 8 == other // 8)
        & (slot % 4 == other % 4)
        & ((other // 4) % 2 <= (slot // 4) % 2)
        & (inner == kv)
    )
    top = jnp.max(jnp.where(visible, scores, FLOOR), axis=1, keepdims=True)
    for i in range(PEERS):
        top = jnp.maximum(top, part_ref[i, :, HD : HD + 1].astype(f32))
    weights = jnp.where(visible, jnp.exp(scores - top), 0.0)
    total = jnp.sum(weights, axis=1, keepdims=True)
    summed = nn_dot(pltpu.roll(weights, 2, 1).astype(bf16), drafts)
    for i in range(PEERS):
        part = part_ref[i].astype(f32)
        factor = jnp.exp(part[:, HD : HD + 1] - top)
        total = total + factor * (part[:, HD + 1 : HD + 2] + part[:, HD + 2 : HD + 3])
        summed = summed + factor * part[:, :HD]
    attn = (summed / total).astype(bf16)
    for i in range(PEERS):
        out_ref[i] = attn


def project_kernel(order_ref, own_ref, oth_ref, w_ref, stream_ref, out_ref, by_slot, by_token):
    kvp = lax.axis_index("kvp")
    core = lax.rem(kvp, 2)
    tp = lax.axis_index("tp")
    acc = jnp.zeros((TOKS, COLS), f32)
    for i in range(HEADS // 2):
        lhs = jnp.concatenate(
            [
                jnp.concatenate([own_ref[2 * i], own_ref[2 * i + 1]], axis=1),
                jnp.concatenate([oth_ref[2 * i], oth_ref[2 * i + 1]], axis=1),
            ],
            axis=0,
        )
        acc = acc + nn_dot(lhs, w_ref[2 * i * HD : (2 * i + 2) * HD, :])
    by_slot[...] = acc
    for r in range(TOKS):
        t = order_ref[lax.rem(r + HALF * core, TOKS)]
        by_token[pl.ds(t, 1), :] = by_slot[r : r + 1, :]
    mine = pl.ds(pl.multiple_of(tp * 16, 16), 16)
    by_token[mine, :] = by_token[mine, :] + stream_ref[...].astype(f32)
    for i in range(NY):
        out_ref[i] = by_token[...]


def norm_kernel(parts_ref, gain_ref, msg_ref, mid_ref, whole):
    tp = lax.axis_index("tp")
    middle = (parts_ref[0] + parts_ref[1]) + (parts_ref[2] + parts_ref[3])
    whole[...] = middle
    mid_ref[...] = whole[pl.ds(pl.multiple_of(tp * 16, 16), 16), :]
    scaled = (middle * gain_ref[...].astype(f32)).astype(bf16)
    squares = jnp.sum(middle * middle, axis=1, keepdims=True)
    high = squares.astype(bf16).astype(f32)
    low = squares - high
    lanes = lane_ids((16, HD))
    stats = jnp.zeros((16, HD), f32)
    for j in range(4):
        stats = jnp.where(lanes == 2 * j, high[16 * j : 16 * j + 16], stats)
        stats = jnp.where(lanes == 2 * j + 1, low[16 * j : 16 * j + 16], stats)
    block = jnp.concatenate(
        [scaled[16 * j : 16 * j + 16] for j in range(4)] + [stats.astype(bf16)], axis=1
    )
    for i in range(PEERS):
        msg_ref[i] = block


def feed_kernel(own_ref, oth_ref, gu_ref, down_ref, send_ref, keep_ref):
    core = lax.rem(lax.axis_index("kvp"), 2)
    gate = jnp.zeros((TOKS, 104), f32)
    up = jnp.zeros((TOKS, 104), f32)
    stats = jnp.zeros((16, HD), f32)
    for i in range(PEERS):
        for src_ref, side in ((own_ref, core), (oth_ref, 1 - core)):
            rows = jnp.concatenate(
                [src_ref[i, :, COLS * j : COLS * (j + 1)] for j in range(4)], axis=0
            )
            cols = pl.ds(pl.multiple_of((2 * i + side) * COLS, COLS), COLS)
            gate = gate + nt_dot(rows, gu_ref[0, :, cols])
            up = up + nt_dot(rows, gu_ref[1, :, cols])
            stats = stats + src_ref[i, :, 4 * COLS :].astype(f32)
    squares = jnp.concatenate(
        [stats[:, 2 * j : 2 * j + 1] + stats[:, 2 * j + 1 : 2 * j + 2] for j in range(4)], axis=0
    )
    rscale = lax.rsqrt(squares / D + EPS)
    gate = gate * rscale
    up = up * rscale
    hidden = (gate / (1.0 + jnp.exp(-gate)) * up).astype(bf16)
    for out_ref, side in ((send_ref, 1 - core), (keep_ref, core)):
        for z in range(NZ):
            for x in range(NX):
                cols = pl.ds(pl.multiple_of((2 * (z * NX + x) + side) * COLS, COLS), COLS)
                part = nn_dot(hidden, down_ref[:, cols]).astype(out_ref.dtype)
                for y in range(NY):
                    out_ref[x * NY + y, z * 16 : (z + 1) * 16, :] = part[16 * y : 16 * y + 16]


VMEM = pl.BlockSpec(memory_space=pltpu.VMEM)
SMEM = pl.BlockSpec(memory_space=pltpu.SMEM)
PARAMS = pltpu.CompilerParams(vmem_limit_bytes=VMEM_LIMIT)


def call(kernel, name, in_specs, out_shape, out_specs, scratch=()):
    return pl.pallas_call(
        kernel,
        name=name,
        in_specs=in_specs,
        out_shape=out_shape,
        out_specs=out_specs,
        scratch_shapes=list(scratch),
        compiler_params=PARAMS,
    )


def on_device(
    query,
    draft_kv,
    key_cache,
    value_cache,
    prompt_of,
    prefix_len,
    out_weight,
    stream,
    norm_gain,
    gate_up,
    down_weight,
):
    shape = jax.ShapeDtypeStruct
    key_pair, value_pair = swap_cores(key_cache), swap_cores(value_cache)
    block = jnp.concatenate(
        [query.reshape(HEADS, HD), draft_kv.reshape(4, HD), jnp.zeros((12, HD), bf16)], axis=0
    )
    own = swap_plane(jnp.broadcast_to(block[None], (PEERS, 48, HD)))
    oth = swap_cores(own)
    part, order = call(
        attention_kernel,
        "attention",
        [SMEM, SMEM, VMEM, VMEM, VMEM, VMEM, VMEM, VMEM],
        [shape((HEADS, HALF, 2 * HD), bf16), shape((TOKS,), jnp.int32)],
        [VMEM, SMEM],
        [pltpu.VMEM((2 * PEERS, 48, HD), bf16), pltpu.SMEM((PROMPTS,), jnp.int32)],
    )(prompt_of, prefix_len, own, oth, key_cache, value_cache, key_pair, value_pair)
    attn = call(
        combine_kernel,
        "combine",
        [SMEM, VMEM, VMEM, VMEM],
        shape((PEERS, HALF, HD), bf16),
        VMEM,
        [pltpu.VMEM((2 * PEERS, 48, HD), bf16)],
    )(order, swap_plane(part), own, oth)
    attn_own = swap_plane(attn)
    attn_oth = swap_cores(attn_own)
    partial = call(
        project_kernel,
        "project",
        [SMEM, VMEM, VMEM, VMEM, VMEM],
        shape((NY, TOKS, COLS), f32),
        VMEM,
        [pltpu.VMEM((TOKS, COLS), f32), pltpu.VMEM((TOKS, COLS), f32)],
    )(order, attn_own, attn_oth, out_weight, stream)
    partial = lax.all_to_all(partial, "tp", 0, 0, tiled=True)
    msg, middle = call(
        norm_kernel,
        "norm",
        [VMEM, VMEM],
        [shape((PEERS, 16, 4 * COLS + HD), bf16), shape((16, COLS), f32)],
        [VMEM, VMEM],
        [pltpu.VMEM((TOKS, COLS), f32)],
    )(partial, norm_gain.reshape(1, COLS))
    normed_own = swap_plane(msg)
    normed_oth = swap_cores(normed_own)
    send, keep = call(
        feed_kernel,
        "feed",
        [VMEM, VMEM, VMEM, VMEM],
        [shape((NX * NY, NZ * 16, COLS), bf16), shape((NX * NY, NZ * 16, COLS), f32)],
        [VMEM, VMEM],
    )(normed_own, normed_oth, gate_up, down_weight)
    summed = (keep + swap_cores(send).astype(f32)).astype(bf16)
    summed = lax.all_to_all(summed, ("kvp", "tp"), 0, 0, axis_index_groups=G_XY, tiled=True)
    summed = jnp.sum(summed.astype(f32), axis=0).astype(bf16).reshape(NZ, 16, COLS)
    summed = lax.all_to_all(summed, "kvp", 0, 0, axis_index_groups=G_Z, tiled=True)
    return (middle + jnp.sum(summed.astype(f32), axis=0)).astype(bf16)


def solution(mesh):
    in_specs = (
        P("kvp", "tp"),
        P("kvp", None, "tp"),
        P(None, "kvp", "tp"),
        P(None, "kvp", "tp"),
        P(),
        P(),
        P("tp", "kvp"),
        P("tp", "kvp"),
        P("kvp"),
        P(None, ("kvp", "tp"), None),
        P(("kvp", "tp"), None),
    )
    out_specs = P("tp", "kvp")
    return jax.shard_map(
        on_device, mesh=mesh, in_specs=in_specs, out_specs=out_specs, check_vma=False
    )
```

```python
import jax
import jax.numpy as jnp
from jax import lax
from jax.experimental import pallas as pl
from jax.experimental.pallas import tpu as pltpu
from jax.sharding import PartitionSpec as P

D = 16384
HD = 128
NZ, NX, NC, NY = 8, 4, 2, 4
PEERS = NZ * NX
HEADS = 32
GROUP = 16
PROMPTS = 8
TOKS = 64
HALF = 32
SHARD = 128
COLS = 256
HIDDEN = 104
EPS = 1e-05
SCALE = HD ** (-0.5)
FLOOR = -1e30
VMEM_LIMIT = 24 * 1024 * 1024

bf16 = jnp.bfloat16
f32 = jnp.float32


def kvp_index(z, x, c):
    return (z * NX + x) * NC + c


def all_index(z, x, c, y):
    return kvp_index(z, x, c) * NY + y


G_XZ = [[kvp_index(z, x, c) for z in range(NZ) for x in range(NX)] for c in range(NC)]
G_Z = [[kvp_index(z, x, c) for z in range(NZ)] for x in range(NX) for c in range(NC)]
G_XY = [
    [all_index(z, x, c, y) for x in range(NX) for y in range(NY)]
    for z in range(NZ)
    for c in range(NC)
]
CORE_PAIRS = [(i, i ^ 1) for i in range(NZ * NX * NC)]


def swap_cores(array):
    return lax.ppermute(array, "kvp", CORE_PAIRS)


def swap_plane(array):
    return lax.all_to_all(array, "kvp", 0, 0, axis_index_groups=G_XZ, tiled=True)


def swap_face(array):
    return lax.all_to_all(array, ("kvp", "tp"), 0, 0, axis_index_groups=G_XY, tiled=True)


def nt_dot(a, b):
    return lax.dot_general(a, b, (((1,), (1,)), ((), ())), preferred_element_type=f32)


def nn_dot(a, b):
    return jnp.dot(a, b, preferred_element_type=f32)


def lane_ids(shape):
    return lax.broadcasted_iota(jnp.int32, shape, len(shape) - 1)


def row_ids(shape):
    return lax.broadcasted_iota(jnp.int32, shape, len(shape) - 2)


def prepare_kernel(
    prompt_ref, len_ref, query_ref, k_ref, v_ref, block_ref, k_out, v_out, order_ref, rows, count, sems
):
    k_copy = pltpu.make_async_copy(k_ref, k_out, sems.at[0])
    v_copy = pltpu.make_async_copy(v_ref, v_out, sems.at[1])
    k_copy.start()
    v_copy.start()
    query = query_ref[...].astype(f32)
    for h in range(HEADS):
        rows[h : h + 1, :] = query[:, h * HD : (h + 1) * HD]
    block = rows[...].astype(bf16)
    for i in range(PEERS):
        block_ref[i] = block
    for p in range(PROMPTS):
        count[p] = 0
        order_ref[TOKS + p] = len_ref[p]
    for s in range(HALF):
        p = prompt_ref[s]
        seen = jnp.minimum(count[p], 3)
        count[p] = seen + 1
        order_ref[p * 8 + seen] = s
        order_ref[p * 8 + 4 + seen] = s + HALF
    k_copy.wait()
    v_copy.wait()


def gather_row(order_ref, slot, core):
    t = order_ref[slot]
    return t // 2 + PEERS * lax.rem(t + core, 2)


def attention_kernel(
    order_ref,
    own_ref,
    oth_ref,
    k_ref,
    v_ref,
    k2_ref,
    v2_ref,
    draft_ref,
    draft2_ref,
    out_ref,
    gath,
    extra,
):
    kvp = lax.axis_index("kvp")
    core = lax.rem(kvp, 2)
    gath[0:PEERS] = own_ref[...]
    gath[PEERS : 2 * PEERS] = oth_ref[...]
    extra[...] = jnp.zeros((GROUP, HD), f32)
    for side, ref in enumerate((draft_ref, draft2_ref)):
        both = ref[0].astype(f32)
        for i in range(4):
            row = side * 4 + i
            extra[row : row + 1, :] = both[i // 2 : i // 2 + 1, (i % 2) * HD : (i % 2 + 1) * HD]
    extras = extra[...]
    to_row = row_ids((256, 256))
    from_row = lane_ids((256, 256))
    regroup = (
        (to_row // GROUP == from_row % GROUP) & (to_row % GROUP == from_row // GROUP)
    ).astype(bf16)
    by_group = (lane_ids((GROUP, SHARD)) % GROUP == row_ids((GROUP, SHARD))).astype(bf16)
    lanes = lane_ids((SHARD, SHARD))
    token = row_ids((SHARD, SHARD)) // GROUP
    here = kvp * SHARD + lanes
    there = (kvp + 1 - 2 * core) * SHARD + lanes
    position = jnp.concatenate([here, there], axis=1)
    for kv in range(2):
        cols = slice(kv * HD, (kv + 1) * HD)
        stats = jnp.zeros((GROUP, SHARD), f32)
        for pair in range(2):
            parts = []
            for q_ in range(2):
                i = pair * 2 + q_
                p = i + 4 * core
                queries = jnp.concatenate(
                    [
                        gath[gather_row(order_ref, p * 8 + j, core), kv * GROUP : (kv + 1) * GROUP, :]
                        for j in range(8)
                    ],
                    axis=0,
                )
                keys = jnp.concatenate([k_ref[p, :, cols], k2_ref[p, :, cols]], axis=0)
                values = jnp.concatenate([v_ref[p, :, cols], v2_ref[p, :, cols]], axis=0)
                scores = nt_dot(queries, keys) * SCALE
                visible = position < order_ref[TOKS + p]
                top = jnp.max(jnp.where(visible, scores, FLOOR), axis=1, keepdims=True)
                top = top.astype(bf16).astype(f32)
                weights = jnp.where(visible, jnp.exp(scores - top), 0.0)
                total = jnp.sum(weights, axis=1, keepdims=True)
                summed = nn_dot(weights.astype(bf16), values)
                parts.append(summed.astype(bf16))
                high = total.astype(bf16).astype(f32)
                low = total - high
                at = token + i * 8
                spread = jnp.where(
                    lanes == at,
                    top,
                    jnp.where(
                        lanes == at + HALF, high, jnp.where(lanes == at + 2 * HALF, low, 0.0)
                    ),
                )
                stats = stats + nn_dot(by_group, spread.astype(bf16))
            both = nn_dot(regroup, jnp.concatenate(parts, axis=0)).astype(bf16)
            for g in range(GROUP):
                out_ref[kv * GROUP + g, pair * 16 : pair * 16 + 16, :] = both[
                    g * 16 : (g + 1) * 16, :
                ]
        inner = row_ids((GROUP, HD))
        for g in range(GROUP):
            out_ref[kv * GROUP + g, HALF : HALF + 16, :] = jnp.where(
                inner == 8, stats[g : g + 1, :], extras
            ).astype(bf16)


def combine_kernel(order_ref, part_ref, gath, out_ref, stat, turn):
    kvp = lax.axis_index("kvp")
    core = lax.rem(kvp, 2)
    head = kvp // 2
    kv = head // GROUP
    first = pl.multiple_of(kv * GROUP, GROUP)
    query_tiles, draft_tiles = [], []
    slots = row_ids((HALF, HD))
    slot_token = jnp.zeros((HALF, HD), jnp.int32)
    for s in range(HALF):
        slot = HALF * core + s
        query_tiles.append(gath[gather_row(order_ref, slot, core), pl.ds(first, GROUP), :])
        slot_token = jnp.where(slots == s, order_ref[slot], slot_token)
    for i in range(PEERS):
        tile = part_ref[i, HALF : HALF + 16, :]
        draft_tiles.append(tile)
        stat[i : i + 1, :] = tile.astype(f32)[8:9, :]
    shape = (HALF, HALF * GROUP)
    outer = lane_ids(shape) // GROUP
    inner = lane_ids(shape) % GROUP
    pick = ((row_ids(shape) == outer) & (inner == head % GROUP)).astype(bf16)
    queries = nn_dot(pick, jnp.concatenate(query_tiles, axis=0)).astype(bf16)
    drafts = jnp.concatenate(draft_tiles, axis=0)
    scores = nt_dot(queries, drafts) * SCALE
    slot_token = jnp.concatenate([slot_token] * 4, axis=1)
    side = inner // 4
    key_token = 2 * outer + jnp.where(side == 0, core, 1 - core)
    visible = (
        (inner % 4 == kv)
        & (side < 2)
        & (slot_token % HALF == key_token % HALF)
        & (key_token // HALF <= slot_token // HALF)
    )
    stats = stat[...]
    top_row = jnp.max(stats, axis=0, keepdims=True)
    factors = jnp.exp(stats - top_row)
    totals = pltpu.roll(stats, HD - HALF, 1) + pltpu.roll(stats, HD - 2 * HALF, 1)
    turn[...] = jnp.zeros((HD, HD), f32)
    turn[0:PEERS, :] = factors
    turn[PEERS : PEERS + 1, :] = jnp.sum(factors * totals, axis=0, keepdims=True)
    turn[PEERS + 1 : PEERS + 2, :] = top_row
    turned = turn[...].T[0:HALF, :]
    total = turned[:, PEERS : PEERS + 1]
    top_cache = turned[:, PEERS + 1 : PEERS + 2]
    summed = jnp.zeros((HALF, HD), f32)
    for i in range(PEERS):
        summed = summed + turned[:, i : i + 1] * part_ref[i, 0:HALF, :].astype(f32)
    top_draft = jnp.max(jnp.where(visible, scores, FLOOR), axis=1, keepdims=True)
    top = jnp.maximum(top_cache, top_draft)
    weights = jnp.where(visible, jnp.exp(scores - top), 0.0)
    scale = jnp.exp(top_cache - top)
    total = scale * total + jnp.sum(weights, axis=1, keepdims=True)
    summed = scale * summed + nn_dot(pltpu.roll(weights, 2, 1).astype(bf16), drafts)
    attn = (summed / total).astype(bf16)
    for i in range(PEERS):
        out_ref[i] = attn


def project_kernel(order_ref, own_ref, oth_ref, w_ref, out_ref, by_slot, by_token):
    core = lax.rem(lax.axis_index("kvp"), 2)
    acc = jnp.zeros((TOKS, COLS), f32)
    for i in range(HEADS // 2):
        lhs = jnp.concatenate(
            [
                jnp.concatenate([own_ref[2 * i], own_ref[2 * i + 1]], axis=1),
                jnp.concatenate([oth_ref[2 * i], oth_ref[2 * i + 1]], axis=1),
            ],
            axis=0,
        )
        acc = acc + nn_dot(lhs, w_ref[2 * i * HD : (2 * i + 2) * HD, :])
    by_slot[...] = acc
    for r in range(TOKS):
        t = order_ref[lax.rem(r + HALF * core, TOKS)]
        by_token[pl.ds(t, 1), :] = by_slot[r : r + 1, :]
    for y in range(NY):
        out_ref[y] = by_token[16 * y : 16 * y + 16, :]


def norm_kernel(parts_ref, stream_ref, gain_ref, msg_ref, mid_ref):
    middle = (
        (parts_ref[0] + parts_ref[1]) + (parts_ref[2] + parts_ref[3])
    ) + stream_ref[...].astype(f32)
    mid_ref[...] = middle
    scaled = (middle * gain_ref[...].astype(f32).reshape(1, COLS)).astype(bf16)
    squares = jnp.sum(middle * middle, axis=1, keepdims=True)
    high = squares.astype(bf16).astype(f32)
    low = squares - high
    lanes = lane_ids((16, HD))
    stats = jnp.where(lanes == 0, high, jnp.where(lanes == 1, low, 0.0)).astype(bf16)
    block = jnp.concatenate([scaled, stats], axis=1)
    for i in range(NZ):
        msg_ref[i] = block


def spread_kernel(in_ref, out_ref):
    stats = jnp.zeros((16, HD), f32)
    for z in range(NZ):
        stats = stats + in_ref[z, :, COLS:].astype(f32)
    squares = stats[:, 0:1] + stats[:, 1:2]
    high = squares.astype(bf16).astype(f32)
    low = squares - high
    lanes = lane_ids((16, COLS))
    tile = jnp.where(lanes == 0, high, jnp.where(lanes == 1, low, 0.0)).astype(bf16)
    for i in range(NX * NY):
        for z in range(NZ):
            out_ref[i, z * 16 : (z + 1) * 16, :] = in_ref[z, :, :COLS]
        out_ref[i, NZ * 16 :, :] = tile


def feed_kernel(own_ref, oth_ref, gu_ref, down_ref, send_ref, keep_ref, weights, sems):
    core = lax.rem(lax.axis_index("kvp"), 2)
    width = D // NZ
    copies = [
        pltpu.make_async_copy(
            gu_ref.at[:, :, pl.ds(z * width, width)], weights.at[z], sems.at[z]
        )
        for z in range(NZ)
    ]
    for copy in copies:
        copy.start()
    gate = jnp.zeros((TOKS, HIDDEN), f32)
    up = jnp.zeros((TOKS, HIDDEN), f32)
    stats = [jnp.zeros((16, HD), f32) for _ in range(NY)]
    for x in range(NX):
        for y in range(NY):
            for src_ref in (own_ref, oth_ref):
                stats[y] = stats[y] + src_ref[x * NY + y, NZ * 16 :, :HD].astype(f32)
    for z in range(NZ):
        copies[z].wait()
        for x in range(NX):
            for src_ref, side in ((own_ref, core), (oth_ref, 1 - core)):
                rows = jnp.concatenate(
                    [src_ref[x * NY + y, z * 16 : (z + 1) * 16, :] for y in range(NY)], axis=0
                )
                cols = pl.ds(pl.multiple_of((2 * x + side) * COLS, COLS), COLS)
                gate = gate + nt_dot(rows, weights[z, 0, :, cols])
                up = up + nt_dot(rows, weights[z, 1, :, cols])
    squares = jnp.concatenate([s[:, 0:1] + s[:, 1:2] for s in stats], axis=0)
    rscale = lax.rsqrt(squares / D + EPS)
    gate = gate * rscale
    up = up * rscale
    hidden = (gate / (1.0 + jnp.exp(-gate)) * up).astype(bf16)
    for out_ref, side in ((send_ref, 1 - core), (keep_ref, core)):
        for z in range(NZ):
            for x in range(NX):
                cols = pl.ds(pl.multiple_of((2 * (z * NX + x) + side) * COLS, COLS), COLS)
                part = nn_dot(hidden, down_ref[:, cols]).astype(out_ref.dtype)
                for y in range(NY):
                    out_ref[x * NY + y, z * 16 : (z + 1) * 16, :] = part[16 * y : 16 * y + 16]


VMEM = pl.BlockSpec(memory_space=pltpu.VMEM)
SMEM = pl.BlockSpec(memory_space=pltpu.SMEM)
HBM = pl.BlockSpec(memory_space=pltpu.HBM)
PARAMS = pltpu.CompilerParams(vmem_limit_bytes=VMEM_LIMIT)


def call(kernel, name, in_specs, out_shape, out_specs, scratch=()):
    return pl.pallas_call(
        kernel,
        name=name,
        in_specs=in_specs,
        out_shape=out_shape,
        out_specs=out_specs,
        scratch_shapes=list(scratch),
        compiler_params=PARAMS,
    )


def in_hbm(array):
    return pltpu.with_memory_space_constraint(array, pltpu.HBM)


def on_device(
    query,
    draft_kv,
    key_cache,
    value_cache,
    prompt_of,
    prefix_len,
    out_weight,
    stream,
    norm_gain,
    gate_up,
    down_weight,
):
    shape = jax.ShapeDtypeStruct
    cache = shape((PROMPTS, SHARD, 2 * HD), bf16)
    key_pair, value_pair = swap_cores(key_cache), swap_cores(value_cache)
    draft_pair = swap_cores(draft_kv)
    block, keys, values, order = call(
        prepare_kernel,
        "prepare",
        [SMEM, SMEM, VMEM, HBM, HBM],
        [
            shape((PEERS, HEADS, HD), bf16),
            cache,
            cache,
            shape((TOKS + PROMPTS,), jnp.int32),
        ],
        [VMEM, VMEM, VMEM, SMEM],
        [
            pltpu.VMEM((HEADS, HD), f32),
            pltpu.SMEM((PROMPTS,), jnp.int32),
            pltpu.SemaphoreType.DMA((2,)),
        ],
    )(in_hbm(prompt_of), in_hbm(prefix_len), in_hbm(query), in_hbm(key_cache), in_hbm(value_cache))
    own = swap_plane(block)
    oth = swap_cores(own)
    part, gath = call(
        attention_kernel,
        "attention",
        [SMEM] + [VMEM] * 8,
        [shape((HEADS, 48, HD), bf16), shape((TOKS, HEADS, HD), bf16)],
        [VMEM, VMEM],
        [pltpu.VMEM((GROUP, HD), f32)],
    )(order, own, oth, keys, values, key_pair, value_pair, draft_kv, draft_pair)
    attn = call(
        combine_kernel,
        "combine",
        [SMEM, VMEM, VMEM],
        shape((PEERS, HALF, HD), bf16),
        VMEM,
        [pltpu.VMEM((PEERS, HD), f32), pltpu.VMEM((HD, HD), f32)],
    )(order, swap_plane(part), gath)
    attn_own = swap_plane(attn)
    attn_oth = swap_cores(attn_own)
    partial = call(
        project_kernel,
        "project",
        [SMEM, VMEM, VMEM, VMEM],
        shape((NY, 16, COLS), f32),
        VMEM,
        [pltpu.VMEM((TOKS, COLS), f32), pltpu.VMEM((TOKS, COLS), f32)],
    )(order, attn_own, attn_oth, out_weight)
    partial = lax.all_to_all(partial, "tp", 0, 0, tiled=True)
    msg, middle = call(
        norm_kernel,
        "norm",
        [VMEM, VMEM, VMEM],
        [shape((NZ, 16, COLS + HD), bf16), shape((16, COLS), f32)],
        [VMEM, VMEM],
    )(partial, in_hbm(stream), in_hbm(norm_gain))
    msg = lax.all_to_all(msg, "kvp", 0, 0, axis_index_groups=G_Z, tiled=True)
    msg = call(spread_kernel, "spread", [VMEM], shape((NX * NY, NZ * 16 + 16, COLS), bf16), VMEM)(
        msg
    )
    normed_own = swap_face(msg)
    normed_oth = swap_cores(normed_own)
    send, keep = call(
        feed_kernel,
        "feed",
        [VMEM, VMEM, HBM, VMEM],
        [shape((NX * NY, NZ * 16, COLS), bf16), shape((NX * NY, NZ * 16, COLS), f32)],
        [VMEM, VMEM],
        [
            pltpu.VMEM((NZ, 2, HIDDEN, D // NZ), bf16),
            pltpu.SemaphoreType.DMA((NZ,)),
        ],
    )(normed_own, normed_oth, in_hbm(gate_up), down_weight)
    summed = (keep + swap_cores(send).astype(f32)).astype(bf16)
    summed = swap_face(summed)
    summed = jnp.sum(summed.astype(f32), axis=0).astype(bf16).reshape(NZ, 16, COLS)
    summed = lax.all_to_all(summed, "kvp", 0, 0, axis_index_groups=G_Z, tiled=True)
    return (middle + jnp.sum(summed.astype(f32), axis=0)).astype(bf16)


def solution(mesh):
    in_specs = (
        P("kvp", "tp"),
        P("kvp", None, "tp"),
        P(None, "kvp", "tp"),
        P(None, "kvp", "tp"),
        P(),
        P(),
        P("tp", "kvp"),
        P("tp", "kvp"),
        P("kvp"),
        P(None, ("kvp", "tp"), None),
        P(("kvp", "tp"), None),
    )
    out_specs = P("tp", "kvp")
    return jax.shard_map(
        on_device, mesh=mesh, in_specs=in_specs, out_specs=out_specs, check_vma=False
    )
```

```python
import jax
import jax.numpy as jnp
from jax import lax
from jax.experimental import pallas as pl
from jax.experimental.pallas import tpu as pltpu
from jax.sharding import PartitionSpec as P

D = 16384
HD = 128
NZ, NX, NC, NY = 8, 4, 2, 4
PEERS = NZ * NX
HEADS = 32
GROUP = 16
PROMPTS = 8
TOKS = 64
HALF = 32
SHARD = 128
COLS = 256
HIDDEN = 104
STAT_ROW = 4
GAIN_ROW = 5
ROWS_OUT = HALF + 8
EPS = 1e-05
SCALE = HD ** (-0.5)
FLOOR = -1e30
VMEM_LIMIT = 18 * 1024 * 1024

bf16 = jnp.bfloat16
f32 = jnp.float32


def kvp_index(z, x, c):
    return (z * NX + x) * NC + c


def all_index(z, x, c, y):
    return kvp_index(z, x, c) * NY + y


G_XZ = [[kvp_index(z, x, c) for z in range(NZ) for x in range(NX)] for c in range(NC)]
G_Z = [[kvp_index(z, x, c) for z in range(NZ)] for x in range(NX) for c in range(NC)]
G_XY = [
    [all_index(z, x, c, y) for x in range(NX) for y in range(NY)]
    for z in range(NZ)
    for c in range(NC)
]
G_YZ = [
    [all_index(z, x, c, y) for z in range(NZ) for y in range(NY)]
    for x in range(NX)
    for c in range(NC)
]
CORE_PAIRS = [(i, i ^ 1) for i in range(NZ * NX * NC)]


def swap_cores(array):
    return lax.ppermute(array, "kvp", CORE_PAIRS)


def swap_plane(array):
    return lax.all_to_all(array, "kvp", 0, 0, axis_index_groups=G_XZ, tiled=True)


def swap_face(array):
    return lax.all_to_all(array, ("kvp", "tp"), 0, 0, axis_index_groups=G_XY, tiled=True)


def nt_dot(a, b):
    return lax.dot_general(a, b, (((1,), (1,)), ((), ())), preferred_element_type=f32)


def nn_dot(a, b):
    return jnp.dot(a, b, preferred_element_type=f32)


def lane_ids(shape):
    return lax.broadcasted_iota(jnp.int32, shape, len(shape) - 1)


def row_ids(shape):
    return lax.broadcasted_iota(jnp.int32, shape, len(shape) - 2)


def prepare_kernel(
    prompt_ref,
    len_ref,
    query_ref,
    draft_ref,
    gain_ref,
    k_ref,
    v_ref,
    block_ref,
    k_out,
    v_out,
    extra_ref,
    order_ref,
    rows,
    count,
    sems,
):
    k_copy = pltpu.make_async_copy(k_ref, k_out, sems.at[0])
    v_copy = pltpu.make_async_copy(v_ref, v_out, sems.at[1])
    k_copy.start()
    v_copy.start()
    query = query_ref[...].astype(f32)
    for h in range(HEADS):
        rows[h : h + 1, :] = query[:, h * HD : (h + 1) * HD]
    block = rows[...].astype(bf16)
    for i in range(PEERS):
        block_ref[i] = block
    extra_ref[...] = jnp.zeros((2, 8, HD), f32)
    gain = gain_ref[...].astype(f32).reshape(1, COLS)
    draft = draft_ref[0].astype(f32)
    for kv in range(2):
        for i in range(2):
            extra_ref[kv, i : i + 1, :] = draft[i : i + 1, kv * HD : (kv + 1) * HD]
            extra_ref[kv, GAIN_ROW + i : GAIN_ROW + i + 1, :] = gain[:, i * HD : (i + 1) * HD]
    for p in range(PROMPTS):
        count[p] = 0
        order_ref[TOKS + p] = len_ref[p]
    for s in range(HALF):
        p = prompt_ref[s]
        seen = jnp.minimum(count[p], 3)
        count[p] = seen + 1
        order_ref[p * 8 + seen] = s
        order_ref[p * 8 + 4 + seen] = s + HALF
    k_copy.wait()
    v_copy.wait()


def gather_row(order_ref, slot, core):
    t = order_ref[slot]
    return t // 2 + PEERS * lax.rem(t + core, 2)


def attention_kernel(
    order_ref,
    own_ref,
    oth_ref,
    k_ref,
    v_ref,
    k2_ref,
    v2_ref,
    extra_ref,
    draft2_ref,
    out_ref,
    gath,
    tail,
):
    kvp = lax.axis_index("kvp")
    core = lax.rem(kvp, 2)
    gath[0:PEERS] = own_ref[...]
    gath[PEERS : 2 * PEERS] = oth_ref[...]
    to_row = row_ids((256, 256))
    from_row = lane_ids((256, 256))
    regroup = (
        (to_row // GROUP == from_row % GROUP) & (to_row % GROUP == from_row // GROUP)
    ).astype(bf16)
    by_group = (lane_ids((GROUP, SHARD)) % GROUP == row_ids((GROUP, SHARD))).astype(bf16)
    lanes = lane_ids((SHARD, SHARD))
    token = row_ids((SHARD, SHARD)) // GROUP
    here = kvp * SHARD + lanes
    there = (kvp + 1 - 2 * core) * SHARD + lanes
    position = jnp.concatenate([here, there], axis=1)
    for kv in range(2):
        cols = slice(kv * HD, (kv + 1) * HD)
        stats = jnp.zeros((GROUP, SHARD), f32)
        for pair in range(2):
            parts = []
            for q_ in range(2):
                i = pair * 2 + q_
                p = i + 4 * core
                queries = jnp.concatenate(
                    [
                        gath[gather_row(order_ref, p * 8 + j, core), kv * GROUP : (kv + 1) * GROUP, :]
                        for j in range(8)
                    ],
                    axis=0,
                )
                keys = jnp.concatenate([k_ref[p, :, cols], k2_ref[p, :, cols]], axis=0)
                values = jnp.concatenate([v_ref[p, :, cols], v2_ref[p, :, cols]], axis=0)
                scores = nt_dot(queries, keys) * SCALE
                visible = position < order_ref[TOKS + p]
                top = jnp.max(jnp.where(visible, scores, FLOOR), axis=1, keepdims=True)
                top = top.astype(bf16).astype(f32)
                weights = jnp.where(visible, jnp.exp(scores - top), 0.0)
                total = jnp.sum(weights, axis=1, keepdims=True)
                summed = nn_dot(weights.astype(bf16), values)
                parts.append(summed.astype(bf16))
                high = total.astype(bf16).astype(f32)
                low = total - high
                at = token + i * 8
                spread = jnp.where(
                    lanes == at,
                    top,
                    jnp.where(
                        lanes == at + HALF, high, jnp.where(lanes == at + 2 * HALF, low, 0.0)
                    ),
                )
                stats = stats + nn_dot(by_group, spread.astype(bf16))
            both = nn_dot(regroup, jnp.concatenate(parts, axis=0)).astype(bf16)
            for g in range(GROUP):
                out_ref[kv * GROUP + g, pair * 16 : pair * 16 + 16, :] = both[
                    g * 16 : (g + 1) * 16, :
                ]
        inner = row_ids((8, HD))
        tail[...] = extra_ref[kv]
        tail[2:4, :] = draft2_ref[0].astype(f32)[:, cols]
        extras = tail[...]
        for g in range(GROUP):
            out_ref[kv * GROUP + g, HALF:ROWS_OUT, :] = jnp.where(
                inner == STAT_ROW, stats[g : g + 1, :], extras
            ).astype(bf16)


def combine_kernel(order_ref, part_ref, gath, out_ref, gain_ref, stat, turn):
    kvp = lax.axis_index("kvp")
    core = lax.rem(kvp, 2)
    head = kvp // 2
    kv = head // GROUP
    first = pl.multiple_of(kv * GROUP, GROUP)
    query_tiles, draft_tiles = [], []
    slots = row_ids((HALF, HD))
    slot_token = jnp.zeros((HALF, HD), jnp.int32)
    for s in range(HALF):
        slot = HALF * core + s
        query_tiles.append(gath[gather_row(order_ref, slot, core), pl.ds(first, GROUP), :])
        slot_token = jnp.where(slots == s, order_ref[slot], slot_token)
    for i in range(PEERS):
        tile = part_ref[i, HALF:ROWS_OUT, :].astype(f32)
        draft_tiles.append(tile)
        stat[i : i + 1, :] = tile[STAT_ROW : STAT_ROW + 1, :]
        for j in range(2):
            gain_ref[i : i + 1, j * HD : (j + 1) * HD] = tile[GAIN_ROW + j : GAIN_ROW + j + 1, :]
    shape = (HALF, HALF * GROUP)
    pick = (
        (row_ids(shape) == lane_ids(shape) // GROUP) & (lane_ids(shape) % GROUP == head % GROUP)
    ).astype(bf16)
    queries = nn_dot(pick, jnp.concatenate(query_tiles, axis=0)).astype(bf16)
    drafts = jnp.concatenate(draft_tiles, axis=0).astype(bf16)
    scores = nt_dot(queries, drafts) * SCALE
    shape = (HALF, PEERS * 8)
    outer = lane_ids(shape) // 8
    inner = lane_ids(shape) % 8
    slot_token = jnp.concatenate([slot_token] * 2, axis=1)
    key_token = 2 * outer + jnp.where(inner == 0, core, 1 - core)
    visible = (
        ((inner == 0) | (inner == 2))
        & (slot_token % HALF == key_token % HALF)
        & (key_token // HALF <= slot_token // HALF)
    )
    stats = stat[...]
    top_row = jnp.max(stats, axis=0, keepdims=True)
    factors = jnp.exp(stats - top_row)
    totals = pltpu.roll(stats, HD - HALF, 1) + pltpu.roll(stats, HD - 2 * HALF, 1)
    turn[...] = jnp.zeros((HD, HD), f32)
    turn[0:PEERS, :] = factors
    turn[PEERS : PEERS + 1, :] = jnp.sum(factors * totals, axis=0, keepdims=True)
    turn[PEERS + 1 : PEERS + 2, :] = top_row
    turned = turn[...].T[0:HALF, :]
    total = turned[:, PEERS : PEERS + 1]
    top_cache = turned[:, PEERS + 1 : PEERS + 2]
    summed = jnp.zeros((HALF, HD), f32)
    for i in range(PEERS):
        summed = summed + turned[:, i : i + 1] * part_ref[i, 0:HALF, :].astype(f32)
    top_draft = jnp.max(jnp.where(visible, scores, FLOOR), axis=1, keepdims=True)
    top = jnp.maximum(top_cache, top_draft)
    weights = jnp.where(visible, jnp.exp(scores - top), 0.0)
    scale = jnp.exp(top_cache - top)
    total = scale * total + jnp.sum(weights, axis=1, keepdims=True)
    summed = scale * summed + nn_dot(pltpu.roll(weights, 1, 1).astype(bf16), drafts)
    attn = (summed / total).astype(bf16)
    for i in range(PEERS):
        out_ref[i] = attn


def project_kernel(order_ref, own_ref, oth_ref, w_ref, stream_ref, out_ref, by_slot, by_token):
    core = lax.rem(lax.axis_index("kvp"), 2)
    tp = lax.axis_index("tp")
    acc = jnp.zeros((TOKS, COLS), f32)
    for i in range(HEADS // 2):
        lhs = jnp.concatenate(
            [
                jnp.concatenate([own_ref[2 * i], own_ref[2 * i + 1]], axis=1),
                jnp.concatenate([oth_ref[2 * i], oth_ref[2 * i + 1]], axis=1),
            ],
            axis=0,
        )
        acc = acc + nn_dot(lhs, w_ref[2 * i * HD : (2 * i + 2) * HD, :])
    by_slot[...] = acc
    for r in range(TOKS):
        t = order_ref[lax.rem(r + HALF * core, TOKS)]
        by_token[pl.ds(t, 1), :] = by_slot[r : r + 1, :]
    mine = pl.ds(pl.multiple_of(tp * 16, 16), 16)
    by_token[mine, :] = by_token[mine, :] + stream_ref[...].astype(f32)
    for y in range(NY):
        rows = by_token[16 * y : 16 * y + 16, :].astype(bf16)
        for z in range(NZ):
            out_ref[z * NY + y] = rows


def spread_kernel(in_ref, gain_ref, out_ref, mid_ref, whole):
    mine = lax.axis_index("kvp") // NC
    x = lax.rem(mine, NX)
    squares = jnp.zeros((16, 1), f32)
    for z in range(NZ):
        parts = [in_ref[z * NY + y].astype(f32) for y in range(NY)]
        middle = (parts[0] + parts[1]) + (parts[2] + parts[3])
        whole[z] = middle
        squares = squares + jnp.sum(middle * middle, axis=1, keepdims=True)
        scaled = (middle * gain_ref[pl.ds(z * NX + x, 1), :]).astype(bf16)
        for i in range(NX * NY):
            out_ref[i, z * 16 : (z + 1) * 16, :] = scaled
    mid_ref[...] = whole[mine // NX]
    high = squares.astype(bf16).astype(f32)
    low = squares - high
    lanes = lane_ids((16, COLS))
    tile = jnp.where(lanes == 0, high, jnp.where(lanes == 1, low, 0.0)).astype(bf16)
    for i in range(NX * NY):
        out_ref[i, NZ * 16 :, :] = tile


def sum_of_squares(src_ref):
    columns = []
    for y in range(NY):
        stats = jnp.zeros((16, HD), f32)
        for x in range(NX):
            stats = stats + src_ref[x * NY + y, NZ * 16 :, :HD].astype(f32)
        columns.append(stats[:, 0:1] + stats[:, 1:2])
    return jnp.concatenate(columns, axis=0)


def token_rows(src_ref, i):
    z, x = i // NX, i % NX
    return jnp.concatenate(
        [src_ref[x * NY + y, z * 16 : (z + 1) * 16, :] for y in range(NY)], axis=0
    )


def gate_kernel(rows_ref, gu_ref, gu2_ref, sums_ref):
    core = lax.rem(lax.axis_index("kvp"), 2)
    sums = [jnp.zeros((TOKS, HIDDEN), f32) for _ in range(4)]
    sums_ref[4] = jnp.broadcast_to(sum_of_squares(rows_ref), (TOKS, HD))
    for i in range(PEERS):
        rows = token_rows(rows_ref, i)
        cols = pl.ds(pl.multiple_of((2 * i + core) * COLS, COLS), COLS)
        for j, ref in enumerate((gu_ref, gu2_ref)):
            for k in range(2):
                sums[2 * j + k] = sums[2 * j + k] + nt_dot(rows, ref[k, :, cols])
    for j in range(4):
        sums_ref[j, :, :HIDDEN] = sums[j]


def down_kernel(own_ref, oth_ref, down_ref, down2_ref, out_ref):
    core = lax.rem(lax.axis_index("kvp"), 2)
    squares = own_ref[4][:, 0:1] + oth_ref[4][:, 0:1]
    rscale = lax.rsqrt(squares / D + EPS)
    hidden = []
    for j in range(2):
        gate = (own_ref[2 * j] + oth_ref[2 - 2 * j])[:, :HIDDEN] * rscale
        up = (own_ref[2 * j + 1] + oth_ref[3 - 2 * j])[:, :HIDDEN] * rscale
        hidden.append((gate / (1.0 + jnp.exp(-gate)) * up).astype(bf16))
    for i in range(PEERS):
        z, x = i // NX, i % NX
        cols = pl.ds(pl.multiple_of((2 * i + core) * COLS, COLS), COLS)
        part = nn_dot(hidden[0], down_ref[:, cols]) + nn_dot(hidden[1], down2_ref[:, cols])
        part = part.astype(bf16)
        for y in range(NY):
            out_ref[x * NY + y, z * 16 : (z + 1) * 16, :] = part[16 * y : 16 * y + 16]


VMEM = pl.BlockSpec(memory_space=pltpu.VMEM)
SMEM = pl.BlockSpec(memory_space=pltpu.SMEM)
HBM = pl.BlockSpec(memory_space=pltpu.HBM)
PARAMS = pltpu.CompilerParams(vmem_limit_bytes=VMEM_LIMIT)


def call(kernel, name, in_specs, out_shape, out_specs, scratch=()):
    return pl.pallas_call(
        kernel,
        name=name,
        in_specs=in_specs,
        out_shape=out_shape,
        out_specs=out_specs,
        scratch_shapes=list(scratch),
        compiler_params=PARAMS,
    )


def in_hbm(array):
    return pltpu.with_memory_space_constraint(array, pltpu.HBM)


def on_device(
    query,
    draft_kv,
    key_cache,
    value_cache,
    prompt_of,
    prefix_len,
    out_weight,
    stream,
    norm_gain,
    gate_up,
    down_weight,
):
    shape = jax.ShapeDtypeStruct
    cache = shape((PROMPTS, SHARD, 2 * HD), bf16)
    key_pair, value_pair = swap_cores(key_cache), swap_cores(value_cache)
    draft_pair = swap_cores(draft_kv)
    block, keys, values, extra, order = call(
        prepare_kernel,
        "prepare",
        [SMEM, SMEM, VMEM, VMEM, VMEM, HBM, HBM],
        [
            shape((PEERS, HEADS, HD), bf16),
            cache,
            cache,
            shape((2, 8, HD), f32),
            shape((TOKS + PROMPTS,), jnp.int32),
        ],
        [VMEM, VMEM, VMEM, VMEM, SMEM],
        [
            pltpu.VMEM((HEADS, HD), f32),
            pltpu.SMEM((PROMPTS,), jnp.int32),
            pltpu.SemaphoreType.DMA((2,)),
        ],
    )(
        in_hbm(prompt_of),
        in_hbm(prefix_len),
        in_hbm(query),
        in_hbm(draft_kv),
        in_hbm(norm_gain),
        in_hbm(key_cache),
        in_hbm(value_cache),
    )
    block, draft_pair, key_pair, value_pair = lax.optimization_barrier(
        (block, draft_pair, key_pair, value_pair)
    )
    own = swap_plane(block)
    oth = swap_cores(own)
    part, gath = call(
        attention_kernel,
        "attention",
        [SMEM] + [VMEM] * 8,
        [shape((HEADS, ROWS_OUT, HD), bf16), shape((TOKS, HEADS, HD), bf16)],
        [VMEM, VMEM],
        [pltpu.VMEM((8, HD), f32)],
    )(order, own, oth, keys, values, key_pair, value_pair, extra, draft_pair)
    part, gate_up_sent = lax.optimization_barrier((part, gate_up))
    gate_up_pair = swap_cores(gate_up_sent)
    attn, gains = call(
        combine_kernel,
        "combine",
        [SMEM, VMEM, VMEM],
        [shape((PEERS, HALF, HD), bf16), shape((PEERS, COLS), f32)],
        [VMEM, VMEM],
        [pltpu.VMEM((PEERS, HD), f32), pltpu.VMEM((HD, HD), f32)],
    )(order, swap_plane(part), gath)
    attn, down_sent = lax.optimization_barrier((attn, down_weight))
    down_pair = swap_cores(down_sent)
    attn_own = swap_plane(attn)
    attn_oth = swap_cores(attn_own)
    partial = call(
        project_kernel,
        "project",
        [SMEM, VMEM, VMEM, VMEM, VMEM],
        shape((NZ * NY, 16, COLS), bf16),
        VMEM,
        [pltpu.VMEM((TOKS, COLS), f32), pltpu.VMEM((TOKS, COLS), f32)],
    )(order, attn_own, attn_oth, out_weight, in_hbm(stream))
    partial = lax.all_to_all(partial, ("kvp", "tp"), 0, 0, axis_index_groups=G_YZ, tiled=True)
    msg, middle = call(
        spread_kernel,
        "spread",
        [VMEM, VMEM],
        [shape((NX * NY, NZ * 16 + 16, COLS), bf16), shape((16, COLS), f32)],
        [VMEM, VMEM],
        [pltpu.VMEM((NZ, 16, COLS), f32)],
    )(partial, gains)
    normed = swap_face(msg)
    sums = call(
        gate_kernel,
        "gate",
        [VMEM] * 3,
        shape((5, TOKS, HD), f32),
        VMEM,
    )(normed, gate_up, gate_up_pair)
    partial = call(
        down_kernel,
        "down",
        [VMEM] * 4,
        shape((NX * NY, NZ * 16, COLS), bf16),
        VMEM,
    )(sums, swap_cores(sums), down_weight, down_pair)
    summed = swap_face(partial)
    summed = jnp.sum(summed.astype(f32), axis=0).astype(bf16).reshape(NZ, 16, COLS)
    summed = lax.all_to_all(summed, "kvp", 0, 0, axis_index_groups=G_Z, tiled=True)
    return (middle + jnp.sum(summed.astype(f32), axis=0)).astype(bf16)


def solution(mesh):
    in_specs = (
        P("kvp", "tp"),
        P("kvp", None, "tp"),
        P(None, "kvp", "tp"),
        P(None, "kvp", "tp"),
        P(),
        P(),
        P("tp", "kvp"),
        P("tp", "kvp"),
        P("kvp"),
        P(None, ("kvp", "tp"), None),
        P(("kvp", "tp"), None),
    )
    out_specs = P("tp", "kvp")
    return jax.shard_map(
        on_device, mesh=mesh, in_specs=in_specs, out_specs=out_specs, check_vma=False
    )
```

```python
import jax
import jax.numpy as jnp
from jax import lax
from jax.experimental import pallas as pl
from jax.experimental.pallas import tpu as pltpu
from jax.sharding import PartitionSpec as P

D = 16384
HD = 128
NZ, NX, NC, NY = 8, 4, 2, 4
PEERS = NZ * NX
HEADS = 32
GROUP = 16
PROMPTS = 8
TOKS = 64
HALF = 32
SHARD = 128
COLS = 256
HIDDEN = 104
STAT_ROW = 4
GAIN_ROW = 5
ROWS_OUT = HALF + 8
EPS = 1e-05
SCALE = HD ** (-0.5)
FLOOR = -1e30
VMEM_LIMIT = 18 * 1024 * 1024

bf16 = jnp.bfloat16
f32 = jnp.float32


def kvp_index(z, x, c):
    return (z * NX + x) * NC + c


def all_index(z, x, c, y):
    return kvp_index(z, x, c) * NY + y


G_XZ = [[kvp_index(z, x, c) for z in range(NZ) for x in range(NX)] for c in range(NC)]
G_Z = [[kvp_index(z, x, c) for z in range(NZ)] for x in range(NX) for c in range(NC)]
G_XY = [
    [all_index(z, x, c, y) for x in range(NX) for y in range(NY)]
    for z in range(NZ)
    for c in range(NC)
]
G_YZ = [
    [all_index(z, x, c, y) for z in range(NZ) for y in range(NY)]
    for x in range(NX)
    for c in range(NC)
]
CORE_PAIRS = [(i, i ^ 1) for i in range(NZ * NX * NC)]


def swap_cores(array):
    return lax.ppermute(array, "kvp", CORE_PAIRS)


def swap_plane(array):
    return lax.all_to_all(array, "kvp", 0, 0, axis_index_groups=G_XZ, tiled=True)


def swap_face(array):
    return lax.all_to_all(array, ("kvp", "tp"), 0, 0, axis_index_groups=G_XY, tiled=True)


def nt_dot(a, b):
    return lax.dot_general(a, b, (((1,), (1,)), ((), ())), preferred_element_type=f32)


def nn_dot(a, b):
    return jnp.dot(a, b, preferred_element_type=f32)


def lane_ids(shape):
    return lax.broadcasted_iota(jnp.int32, shape, len(shape) - 1)


def row_ids(shape):
    return lax.broadcasted_iota(jnp.int32, shape, len(shape) - 2)


def prepare_kernel(
    prompt_ref,
    len_ref,
    query_ref,
    draft_ref,
    gain_ref,
    k_ref,
    v_ref,
    block_ref,
    k_out,
    v_out,
    extra_ref,
    order_ref,
    rows,
    count,
    sems,
):
    half = pl.ds(lax.rem(lax.axis_index("kvp"), 2) * (PROMPTS // 2), PROMPTS // 2)
    k_copy = pltpu.make_async_copy(k_ref.at[half], k_out, sems.at[0])
    v_copy = pltpu.make_async_copy(v_ref.at[half], v_out, sems.at[1])
    k_copy.start()
    v_copy.start()
    query = query_ref[...].astype(f32)
    for h in range(HEADS):
        rows[h : h + 1, :] = query[:, h * HD : (h + 1) * HD]
    block = rows[...].astype(bf16)
    for i in range(PEERS):
        block_ref[i] = block
    extra_ref[...] = jnp.zeros((2, 8, HD), f32)
    gain = gain_ref[...].astype(f32).reshape(1, COLS)
    draft = draft_ref[0].astype(f32)
    for kv in range(2):
        for i in range(2):
            extra_ref[kv, i : i + 1, :] = draft[i : i + 1, kv * HD : (kv + 1) * HD]
            extra_ref[kv, GAIN_ROW + i : GAIN_ROW + i + 1, :] = gain[:, i * HD : (i + 1) * HD]
    for p in range(PROMPTS):
        count[p] = 0
        order_ref[TOKS + p] = len_ref[p]
    for s in range(HALF):
        p = prompt_ref[s]
        seen = jnp.minimum(count[p], 3)
        count[p] = seen + 1
        order_ref[p * 8 + seen] = s
        order_ref[p * 8 + 4 + seen] = s + HALF
    k_copy.wait()
    v_copy.wait()


def gather_row(order_ref, slot, core):
    t = order_ref[slot]
    return t // 2 + PEERS * lax.rem(t + core, 2)


def attention_kernel(
    order_ref,
    own_ref,
    oth_ref,
    k_ref,
    v_ref,
    k2_ref,
    v2_ref,
    extra_ref,
    draft2_ref,
    out_ref,
    query_ref,
    slot_ref,
    lane_ref,
    gath,
    tail,
):
    kvp = lax.axis_index("kvp")
    core = lax.rem(kvp, 2)
    gath[0:PEERS] = own_ref[...]
    gath[PEERS : 2 * PEERS] = oth_ref[...]
    to_row = row_ids((256, 256))
    from_row = lane_ids((256, 256))
    regroup = (
        (to_row // GROUP == from_row % GROUP) & (to_row % GROUP == from_row // GROUP)
    ).astype(bf16)
    by_group = (lane_ids((GROUP, SHARD)) % GROUP == row_ids((GROUP, SHARD))).astype(bf16)
    lanes = lane_ids((SHARD, SHARD))
    token = row_ids((SHARD, SHARD)) // GROUP
    here = kvp * SHARD + lanes
    there = (kvp + 1 - 2 * core) * SHARD + lanes
    position = jnp.concatenate([here, there], axis=1)
    slots = row_ids((HALF, HD))
    slot_token = jnp.zeros((HALF, HD), jnp.int32)
    for s in range(HALF):
        slot_token = jnp.where(slots == s, order_ref[HALF * core + s], slot_token)
    slot_ref[...] = slot_token
    row = lane_ids((8, HD))
    row_token = jnp.full((8, HD), -1, jnp.int32)
    for r in range(TOKS):
        row_token = jnp.where(row == r, order_ref[lax.rem(r + HALF * core, TOKS)], row_token)
    lane_ref[...] = row_token
    for kv in range(2):
        cols = slice(kv * HD, (kv + 1) * HD)
        stats = jnp.zeros((GROUP, SHARD), f32)
        for pair in range(2):
            parts = []
            for q_ in range(2):
                i = pair * 2 + q_
                p = i + 4 * core
                tiles = [
                    gath[gather_row(order_ref, p * 8 + j, core), kv * GROUP : (kv + 1) * GROUP, :]
                    for j in range(8)
                ]
                for j in range(8):
                    query_ref[i * 8 + j, kv * GROUP : (kv + 1) * GROUP, :] = tiles[j]
                queries = jnp.concatenate(tiles, axis=0)
                keys = jnp.concatenate([k_ref[i, :, cols], k2_ref[p, :, cols]], axis=0)
                values = jnp.concatenate([v_ref[i, :, cols], v2_ref[p, :, cols]], axis=0)
                scores = nt_dot(queries, keys) * SCALE
                visible = position < order_ref[TOKS + p]
                top = jnp.max(jnp.where(visible, scores, FLOOR), axis=1, keepdims=True)
                top = top.astype(bf16).astype(f32)
                weights = jnp.where(visible, jnp.exp(scores - top), 0.0)
                total = jnp.sum(weights, axis=1, keepdims=True)
                summed = nn_dot(weights.astype(bf16), values)
                parts.append(summed.astype(bf16))
                high = total.astype(bf16).astype(f32)
                low = total - high
                at = token + i * 8
                spread = jnp.where(
                    lanes == at,
                    top,
                    jnp.where(
                        lanes == at + HALF, high, jnp.where(lanes == at + 2 * HALF, low, 0.0)
                    ),
                )
                stats = stats + nn_dot(by_group, spread.astype(bf16))
            both = nn_dot(regroup, jnp.concatenate(parts, axis=0)).astype(bf16)
            for g in range(GROUP):
                out_ref[kv * GROUP + g, pair * 16 : pair * 16 + 16, :] = both[
                    g * 16 : (g + 1) * 16, :
                ]
        inner = row_ids((8, HD))
        tail[...] = extra_ref[kv]
        tail[2:4, :] = draft2_ref[0].astype(f32)[:, cols]
        extras = tail[...]
        for g in range(GROUP):
            out_ref[kv * GROUP + g, HALF:ROWS_OUT, :] = jnp.where(
                inner == STAT_ROW, stats[g : g + 1, :], extras
            ).astype(bf16)


def combine_kernel(part_ref, query_ref, slot_ref, out_ref, gain_ref, stat, turn):
    kvp = lax.axis_index("kvp")
    core = lax.rem(kvp, 2)
    head = kvp // 2
    kv = head // GROUP
    first = pl.multiple_of(kv * GROUP, GROUP)
    slot_token = slot_ref[...]
    query_tiles = [query_ref[s, pl.ds(first, GROUP), :] for s in range(HALF)]
    draft_tiles = []
    for i in range(PEERS):
        tile = part_ref[i, HALF:ROWS_OUT, :].astype(f32)
        draft_tiles.append(tile)
        stat[i : i + 1, :] = tile[STAT_ROW : STAT_ROW + 1, :]
        for j in range(2):
            gain_ref[i : i + 1, j * HD : (j + 1) * HD] = tile[GAIN_ROW + j : GAIN_ROW + j + 1, :]
    shape = (HALF, HALF * GROUP)
    pick = (
        (row_ids(shape) == lane_ids(shape) // GROUP) & (lane_ids(shape) % GROUP == head % GROUP)
    ).astype(bf16)
    queries = nn_dot(pick, jnp.concatenate(query_tiles, axis=0)).astype(bf16)
    drafts = jnp.concatenate(draft_tiles, axis=0).astype(bf16)
    scores = nt_dot(queries, drafts) * SCALE
    shape = (HALF, PEERS * 8)
    outer = lane_ids(shape) // 8
    inner = lane_ids(shape) % 8
    slot_token = jnp.concatenate([slot_token] * 2, axis=1)
    key_token = 2 * outer + jnp.where(inner == 0, core, 1 - core)
    visible = (
        ((inner == 0) | (inner == 2))
        & (slot_token % HALF == key_token % HALF)
        & (key_token // HALF <= slot_token // HALF)
    )
    stats = stat[...]
    top_row = jnp.max(stats, axis=0, keepdims=True)
    factors = jnp.exp(stats - top_row)
    totals = pltpu.roll(stats, HD - HALF, 1) + pltpu.roll(stats, HD - 2 * HALF, 1)
    turn[...] = jnp.zeros((HD, HD), f32)
    turn[0:PEERS, :] = factors
    turn[PEERS : PEERS + 1, :] = jnp.sum(factors * totals, axis=0, keepdims=True)
    turn[PEERS + 1 : PEERS + 2, :] = top_row
    turned = turn[...].T[0:HALF, :]
    total = turned[:, PEERS : PEERS + 1]
    top_cache = turned[:, PEERS + 1 : PEERS + 2]
    summed = jnp.zeros((HALF, HD), f32)
    for i in range(PEERS):
        summed = summed + turned[:, i : i + 1] * part_ref[i, 0:HALF, :].astype(f32)
    top_draft = jnp.max(jnp.where(visible, scores, FLOOR), axis=1, keepdims=True)
    top = jnp.maximum(top_cache, top_draft)
    weights = jnp.where(visible, jnp.exp(scores - top), 0.0)
    scale = jnp.exp(top_cache - top)
    total = scale * total + jnp.sum(weights, axis=1, keepdims=True)
    summed = scale * summed + nn_dot(pltpu.roll(weights, 1, 1).astype(bf16), drafts)
    attn = (summed / total).astype(bf16)
    for i in range(PEERS):
        out_ref[i] = attn


def project_kernel(token_ref, own_ref, oth_ref, w_ref, stream_ref, out_ref, by_token):
    tp = lax.axis_index("tp")
    acc = jnp.zeros((TOKS, COLS), f32)
    for i in range(HEADS // 2):
        lhs = jnp.concatenate(
            [
                jnp.concatenate([own_ref[2 * i], own_ref[2 * i + 1]], axis=1),
                jnp.concatenate([oth_ref[2 * i], oth_ref[2 * i + 1]], axis=1),
            ],
            axis=0,
        )
        acc = acc + nn_dot(lhs, w_ref[2 * i * HD : (2 * i + 2) * HD, :])
    place = (row_ids((TOKS, HD)) == token_ref[0:1, :]).astype(bf16)[:, :TOKS]
    high = acc.astype(bf16)
    rest = acc - high.astype(f32)
    middle = rest.astype(bf16)
    low = (rest - middle.astype(f32)).astype(bf16)
    by_token[...] = nn_dot(place, high) + (nn_dot(place, middle) + nn_dot(place, low))
    mine = pl.ds(pl.multiple_of(tp * 16, 16), 16)
    by_token[mine, :] = by_token[mine, :] + stream_ref[...].astype(f32)
    for y in range(NY):
        rows = by_token[16 * y : 16 * y + 16, :].astype(bf16)
        for z in range(NZ):
            out_ref[z * NY + y] = rows


def spread_kernel(in_ref, gain_ref, out_ref, mid_ref, whole):
    mine = lax.axis_index("kvp") // NC
    x = lax.rem(mine, NX)
    for z in range(NZ):
        parts = [in_ref[z * NY + y].astype(f32) for y in range(NY)]
        middle = (parts[0] + parts[1]) + (parts[2] + parts[3])
        whole[z] = middle
        scaled = (middle * gain_ref[pl.ds(z * NX + x, 1), :]).astype(bf16)
        for i in range(NX * NY):
            out_ref[i, z * 16 : (z + 1) * 16, :] = scaled
    mid_ref[...] = whole[mine // NX]


def token_rows(src_ref, i):
    z, x = i // NX, i % NX
    return jnp.concatenate(
        [src_ref[x * NY + y, z * 16 : (z + 1) * 16, :] for y in range(NY)], axis=0
    )


def gate_kernel(rows_ref, gain_ref, gu_ref, gu2_ref, sums_ref):
    core = lax.rem(lax.axis_index("kvp"), 2)
    sums = [jnp.zeros((TOKS, 2 * HIDDEN), f32) for _ in range(2)]
    squares = jnp.zeros((TOKS, COLS), f32)
    inverse = 1.0 / gain_ref[...]
    for i in range(PEERS):
        rows = token_rows(rows_ref, i)
        middle = rows.astype(f32) * inverse[i : i + 1, :]
        squares = squares + middle * middle
        cols = pl.ds(pl.multiple_of((2 * i + core) * COLS, COLS), COLS)
        for j, ref in enumerate((gu_ref, gu2_ref)):
            both = jnp.concatenate([ref[0, :, cols], ref[1, :, cols]], axis=0)
            sums[j] = sums[j] + nt_dot(rows, both)
    for j in range(2):
        sums_ref[j, :, : 2 * HIDDEN] = sums[j]
    sums_ref[2] = jnp.broadcast_to(jnp.sum(squares, axis=1, keepdims=True), (TOKS, COLS))


def down_kernel(own_ref, oth_ref, down_ref, down2_ref, out_ref):
    core = lax.rem(lax.axis_index("kvp"), 2)
    squares = own_ref[2][:, 0:1] + oth_ref[2][:, 0:1]
    rscale = lax.rsqrt(squares / D + EPS)
    hidden = []
    for j in range(2):
        total = (own_ref[j] + oth_ref[1 - j]) * rscale
        gate, up = total[:, :HIDDEN], total[:, HIDDEN : 2 * HIDDEN]
        hidden.append((gate / (1.0 + jnp.exp(-gate)) * up).astype(bf16))
    for i in range(PEERS):
        z, x = i // NX, i % NX
        cols = pl.ds(pl.multiple_of((2 * i + core) * COLS, COLS), COLS)
        part = nn_dot(hidden[0], down_ref[:, cols]) + nn_dot(hidden[1], down2_ref[:, cols])
        part = part.astype(bf16)
        for y in range(NY):
            out_ref[x * NY + y, z * 16 : (z + 1) * 16, :] = part[16 * y : 16 * y + 16]


VMEM = pl.BlockSpec(memory_space=pltpu.VMEM)
SMEM = pl.BlockSpec(memory_space=pltpu.SMEM)
HBM = pl.BlockSpec(memory_space=pltpu.HBM)
COST = pl.CostEstimate(flops=10**9, bytes_accessed=4 * 10**7, transcendentals=0)
PARAMS = pltpu.CompilerParams(vmem_limit_bytes=VMEM_LIMIT)


def call(kernel, name, in_specs, out_shape, out_specs, scratch=(), cost=COST):
    return pl.pallas_call(
        kernel,
        name=name,
        in_specs=in_specs,
        out_shape=out_shape,
        out_specs=out_specs,
        scratch_shapes=list(scratch),
        compiler_params=PARAMS,
        cost_estimate=cost,
    )


def in_hbm(array):
    return pltpu.with_memory_space_constraint(array, pltpu.HBM)


def on_device(
    query,
    draft_kv,
    key_cache,
    value_cache,
    prompt_of,
    prefix_len,
    out_weight,
    stream,
    norm_gain,
    gate_up,
    down_weight,
):
    shape = jax.ShapeDtypeStruct
    cache = shape((PROMPTS // 2, SHARD, 2 * HD), bf16)
    key_pair, value_pair = swap_cores(key_cache), swap_cores(value_cache)
    draft_pair = swap_cores(draft_kv)
    block, keys, values, extra, order = call(
        prepare_kernel,
        "prepare",
        [SMEM, SMEM, VMEM, VMEM, VMEM, HBM, HBM],
        [
            shape((PEERS, HEADS, HD), bf16),
            cache,
            cache,
            shape((2, 8, HD), f32),
            shape((TOKS + PROMPTS,), jnp.int32),
        ],
        [VMEM, VMEM, VMEM, VMEM, SMEM],
        [
            pltpu.VMEM((HEADS, HD), f32),
            pltpu.SMEM((PROMPTS,), jnp.int32),
            pltpu.SemaphoreType.DMA((2,)),
        ],
        None,
    )(
        in_hbm(prompt_of),
        in_hbm(prefix_len),
        in_hbm(query),
        in_hbm(draft_kv),
        in_hbm(norm_gain),
        in_hbm(key_cache),
        in_hbm(value_cache),
    )
    block, draft_pair, key_pair, value_pair = lax.optimization_barrier(
        (block, draft_pair, key_pair, value_pair)
    )
    own = swap_plane(block)
    oth = swap_cores(own)
    part, queries, slot_token, row_token = call(
        attention_kernel,
        "attention",
        [SMEM] + [VMEM] * 8,
        [
            shape((HEADS, ROWS_OUT, HD), bf16),
            shape((HALF, HEADS, HD), bf16),
            shape((HALF, HD), jnp.int32),
            shape((8, HD), jnp.int32),
        ],
        [VMEM] * 4,
        [pltpu.VMEM((TOKS, HEADS, HD), bf16), pltpu.VMEM((8, HD), f32)],
    )(
        order,
        own,
        oth,
        keys,
        values,
        key_pair,
        value_pair,
        extra,
        draft_pair,
    )
    part, gate_up_sent = lax.optimization_barrier((part, gate_up))
    gate_up_pair = swap_cores(gate_up_sent)
    attn, gains = call(
        combine_kernel,
        "combine",
        [VMEM, VMEM, VMEM],
        [shape((PEERS, HALF, HD), bf16), shape((PEERS, COLS), f32)],
        [VMEM, VMEM],
        [pltpu.VMEM((PEERS, HD), f32), pltpu.VMEM((HD, HD), f32)],
    )(swap_plane(part), queries, slot_token)
    attn, down_sent = lax.optimization_barrier((attn, down_weight))
    down_pair = swap_cores(down_sent)
    attn_own = swap_plane(attn)
    attn_oth = swap_cores(attn_own)
    partial = call(
        project_kernel,
        "project",
        [VMEM] * 5,
        shape((NZ * NY, 16, COLS), bf16),
        VMEM,
        [pltpu.VMEM((TOKS, COLS), f32)],
    )(row_token, attn_own, attn_oth, out_weight, in_hbm(stream))
    partial = lax.all_to_all(partial, ("kvp", "tp"), 0, 0, axis_index_groups=G_YZ, tiled=True)
    msg, middle = call(
        spread_kernel,
        "spread",
        [VMEM, VMEM],
        [shape((NX * NY, NZ * 16, COLS), bf16), shape((16, COLS), f32)],
        [VMEM, VMEM],
        [pltpu.VMEM((NZ, 16, COLS), f32)],
    )(partial, gains)
    normed = swap_face(msg)
    sums = call(
        gate_kernel,
        "gate",
        [VMEM] * 4,
        shape((3, TOKS, COLS), f32),
        VMEM,
    )(normed, gains, gate_up, gate_up_pair)
    partial = call(
        down_kernel,
        "down",
        [VMEM] * 4,
        shape((NX * NY, NZ * 16, COLS), bf16),
        VMEM,
    )(sums, swap_cores(sums), down_weight, down_pair)
    summed = swap_face(partial)
    summed = jnp.sum(summed.astype(f32), axis=0).astype(bf16).reshape(NZ, 16, COLS)
    summed = lax.all_to_all(summed, "kvp", 0, 0, axis_index_groups=G_Z, tiled=True)
    return (middle + jnp.sum(summed.astype(f32), axis=0)).astype(bf16)


def solution(mesh):
    in_specs = (
        P("kvp", "tp"),
        P("kvp", None, "tp"),
        P(None, "kvp", "tp"),
        P(None, "kvp", "tp"),
        P(),
        P(),
        P("tp", "kvp"),
        P("tp", "kvp"),
        P("kvp"),
        P(None, ("kvp", "tp"), None),
        P(("kvp", "tp"), None),
    )
    out_specs = P("tp", "kvp")
    return jax.shard_map(
        on_device, mesh=mesh, in_specs=in_specs, out_specs=out_specs, check_vma=False
    )
```

```python
import jax
import jax.numpy as jnp
from jax import lax
from jax.experimental import pallas as pl
from jax.experimental.pallas import tpu as pltpu
from jax.sharding import PartitionSpec as P

D = 16384
HD = 128
NZ, NX, NC, NY = 8, 4, 2, 4
PEERS = NZ * NX
HEADS = 32
GROUP = 16
PROMPTS = 8
TOKS = 64
HALF = 32
SHARD = 128
COLS = 256
HIDDEN = 104
STAT_ROW = 4
GAIN_ROW = 5
ROWS_OUT = HALF + 8
EPS = 1e-05
SCALE = HD ** (-0.5)
FLOOR = -1e30
VMEM_LIMIT = 18 * 1024 * 1024

bf16 = jnp.bfloat16
f32 = jnp.float32


def kvp_index(z, x, c):
    return (z * NX + x) * NC + c


def all_index(z, x, c, y):
    return kvp_index(z, x, c) * NY + y


G_XZ = [[kvp_index(z, x, c) for z in range(NZ) for x in range(NX)] for c in range(NC)]
G_Z = [[kvp_index(z, x, c) for z in range(NZ)] for x in range(NX) for c in range(NC)]
G_XY = [
    [all_index(z, x, c, y) for x in range(NX) for y in range(NY)]
    for z in range(NZ)
    for c in range(NC)
]
G_YZ = [
    [all_index(z, x, c, y) for z in range(NZ) for y in range(NY)]
    for x in range(NX)
    for c in range(NC)
]
G_LINE = [[all_index(z, x, 0, y) for x in range(NX)] for z in range(NZ) for y in range(NY)] + [
    [all_index(z, x, 1, y) for y in range(NY)] for z in range(NZ) for x in range(NX)
]
G_REST = [[all_index(z, x, 0, y) for y in range(NY) for z in range(NZ)] for x in range(NX)] + [
    [all_index(z, x, 1, y) for x in range(NX) for z in range(NZ)] for y in range(NY)
]
CORE_PAIRS = [(i, i ^ 1) for i in range(NZ * NX * NC)]


def swap_cores(array):
    return lax.ppermute(array, "kvp", CORE_PAIRS)


def swap_plane(array):
    return lax.all_to_all(array, "kvp", 0, 0, axis_index_groups=G_XZ, tiled=True)


def swap_face(array):
    return lax.all_to_all(array, ("kvp", "tp"), 0, 0, axis_index_groups=G_XY, tiled=True)


def nt_dot(a, b):
    return lax.dot_general(a, b, (((1,), (1,)), ((), ())), preferred_element_type=f32)


def nn_dot(a, b):
    return jnp.dot(a, b, preferred_element_type=f32)


def lane_ids(shape):
    return lax.broadcasted_iota(jnp.int32, shape, len(shape) - 1)


def row_ids(shape):
    return lax.broadcasted_iota(jnp.int32, shape, len(shape) - 2)


def prepare_kernel(
    prompt_ref,
    len_ref,
    query_ref,
    draft_ref,
    gain_ref,
    k_ref,
    v_ref,
    block_ref,
    k_out,
    v_out,
    extra_ref,
    order_ref,
    rows,
    count,
    sems,
):
    half = pl.ds(lax.rem(lax.axis_index("kvp"), 2) * (PROMPTS // 2), PROMPTS // 2)
    k_copy = pltpu.make_async_copy(k_ref.at[half], k_out, sems.at[0])
    v_copy = pltpu.make_async_copy(v_ref.at[half], v_out, sems.at[1])
    k_copy.start()
    v_copy.start()
    query = query_ref[...].astype(f32)
    for h in range(HEADS):
        rows[h : h + 1, :] = query[:, h * HD : (h + 1) * HD]
    block = rows[...].astype(bf16)
    for i in range(PEERS):
        block_ref[i] = block
    extra_ref[...] = jnp.zeros((2, 8, HD), f32)
    gain = gain_ref[...].astype(f32).reshape(1, COLS)
    draft = draft_ref[0].astype(f32)
    for kv in range(2):
        for i in range(2):
            extra_ref[kv, i : i + 1, :] = draft[i : i + 1, kv * HD : (kv + 1) * HD]
            extra_ref[kv, GAIN_ROW + i : GAIN_ROW + i + 1, :] = gain[:, i * HD : (i + 1) * HD]
    for p in range(PROMPTS):
        count[p] = 0
        order_ref[TOKS + p] = len_ref[p]
    for s in range(HALF):
        p = prompt_ref[s]
        seen = jnp.minimum(count[p], 3)
        count[p] = seen + 1
        order_ref[p * 8 + seen] = s
        order_ref[p * 8 + 4 + seen] = s + HALF
    k_copy.wait()
    v_copy.wait()


def gather_row(order_ref, slot, core):
    t = order_ref[slot]
    return t // 2 + PEERS * lax.rem(t + core, 2)


def attention_kernel(
    order_ref,
    own_ref,
    oth_ref,
    k_ref,
    v_ref,
    k2_ref,
    v2_ref,
    extra_ref,
    draft2_ref,
    out_ref,
    query_ref,
    slot_ref,
    lane_ref,
    gath,
    tail,
):
    kvp = lax.axis_index("kvp")
    core = lax.rem(kvp, 2)
    gath[0:PEERS] = own_ref[...]
    gath[PEERS : 2 * PEERS] = oth_ref[...]
    to_row = row_ids((256, 256))
    from_row = lane_ids((256, 256))
    regroup = (
        (to_row // GROUP == from_row % GROUP) & (to_row % GROUP == from_row // GROUP)
    ).astype(bf16)
    by_group = (lane_ids((GROUP, SHARD)) % GROUP == row_ids((GROUP, SHARD))).astype(bf16)
    lanes = lane_ids((SHARD, SHARD))
    token = row_ids((SHARD, SHARD)) // GROUP
    here = kvp * SHARD + lanes
    there = (kvp + 1 - 2 * core) * SHARD + lanes
    position = jnp.concatenate([here, there], axis=1)
    slots = row_ids((HALF, HD))
    slot_token = jnp.zeros((HALF, HD), jnp.int32)
    for s in range(HALF):
        slot_token = jnp.where(slots == s, order_ref[HALF * core + s], slot_token)
    slot_ref[...] = slot_token
    row = lane_ids((8, HD))
    row_token = jnp.full((8, HD), -1, jnp.int32)
    for r in range(TOKS):
        row_token = jnp.where(row == r, order_ref[lax.rem(r + HALF * core, TOKS)], row_token)
    lane_ref[...] = row_token
    for kv in range(2):
        cols = slice(kv * HD, (kv + 1) * HD)
        stats = jnp.zeros((GROUP, SHARD), f32)
        for pair in range(2):
            parts = []
            for q_ in range(2):
                i = pair * 2 + q_
                p = i + 4 * core
                tiles = [
                    gath[gather_row(order_ref, p * 8 + j, core), kv * GROUP : (kv + 1) * GROUP, :]
                    for j in range(8)
                ]
                for j in range(8):
                    query_ref[i * 8 + j, kv * GROUP : (kv + 1) * GROUP, :] = tiles[j]
                queries = jnp.concatenate(tiles, axis=0)
                keys = jnp.concatenate([k_ref[i, :, cols], k2_ref[p, :, cols]], axis=0)
                values = jnp.concatenate([v_ref[i, :, cols], v2_ref[p, :, cols]], axis=0)
                scores = nt_dot(queries, keys) * SCALE
                visible = position < order_ref[TOKS + p]
                top = jnp.max(jnp.where(visible, scores, FLOOR), axis=1, keepdims=True)
                top = top.astype(bf16).astype(f32)
                weights = jnp.where(visible, jnp.exp(scores - top), 0.0)
                total = jnp.sum(weights, axis=1, keepdims=True)
                summed = nn_dot(weights.astype(bf16), values)
                parts.append(summed.astype(bf16))
                high = total.astype(bf16).astype(f32)
                low = total - high
                at = token + i * 8
                spread = jnp.where(
                    lanes == at,
                    top,
                    jnp.where(
                        lanes == at + HALF, high, jnp.where(lanes == at + 2 * HALF, low, 0.0)
                    ),
                )
                stats = stats + nn_dot(by_group, spread.astype(bf16))
            both = nn_dot(regroup, jnp.concatenate(parts, axis=0)).astype(bf16)
            for g in range(GROUP):
                out_ref[kv * GROUP + g, pair * 16 : pair * 16 + 16, :] = both[
                    g * 16 : (g + 1) * 16, :
                ]
        inner = row_ids((8, HD))
        tail[...] = extra_ref[kv]
        tail[2:4, :] = draft2_ref[0].astype(f32)[:, cols]
        extras = tail[...]
        for g in range(GROUP):
            out_ref[kv * GROUP + g, HALF:ROWS_OUT, :] = jnp.where(
                inner == STAT_ROW, stats[g : g + 1, :], extras
            ).astype(bf16)


def combine_kernel(part_ref, query_ref, slot_ref, out_ref, gain_ref, stat, turn):
    kvp = lax.axis_index("kvp")
    core = lax.rem(kvp, 2)
    head = kvp // 2
    kv = head // GROUP
    first = pl.multiple_of(kv * GROUP, GROUP)
    slot_token = slot_ref[...]
    query_tiles = [query_ref[s, pl.ds(first, GROUP), :] for s in range(HALF)]
    draft_tiles = []
    for i in range(PEERS):
        tile = part_ref[i, HALF:ROWS_OUT, :].astype(f32)
        draft_tiles.append(tile)
        stat[i : i + 1, :] = tile[STAT_ROW : STAT_ROW + 1, :]
        for j in range(2):
            gain_ref[i : i + 1, j * HD : (j + 1) * HD] = tile[GAIN_ROW + j : GAIN_ROW + j + 1, :]
    shape = (HALF, HALF * GROUP)
    pick = (
        (row_ids(shape) == lane_ids(shape) // GROUP) & (lane_ids(shape) % GROUP == head % GROUP)
    ).astype(bf16)
    queries = nn_dot(pick, jnp.concatenate(query_tiles, axis=0)).astype(bf16)
    drafts = jnp.concatenate(draft_tiles, axis=0).astype(bf16)
    scores = nt_dot(queries, drafts) * SCALE
    shape = (HALF, PEERS * 8)
    outer = lane_ids(shape) // 8
    inner = lane_ids(shape) % 8
    slot_token = jnp.concatenate([slot_token] * 2, axis=1)
    key_token = 2 * outer + jnp.where(inner == 0, core, 1 - core)
    visible = (
        ((inner == 0) | (inner == 2))
        & (slot_token % HALF == key_token % HALF)
        & (key_token // HALF <= slot_token // HALF)
    )
    stats = stat[...]
    top_row = jnp.max(stats, axis=0, keepdims=True)
    factors = jnp.exp(stats - top_row)
    totals = pltpu.roll(stats, HD - HALF, 1) + pltpu.roll(stats, HD - 2 * HALF, 1)
    turn[...] = jnp.zeros((HD, HD), f32)
    turn[0:PEERS, :] = factors
    turn[PEERS : PEERS + 1, :] = jnp.sum(factors * totals, axis=0, keepdims=True)
    turn[PEERS + 1 : PEERS + 2, :] = top_row
    turned = turn[...].T[0:HALF, :]
    total = turned[:, PEERS : PEERS + 1]
    top_cache = turned[:, PEERS + 1 : PEERS + 2]
    summed = jnp.zeros((HALF, HD), f32)
    for i in range(PEERS):
        summed = summed + turned[:, i : i + 1] * part_ref[i, 0:HALF, :].astype(f32)
    top_draft = jnp.max(jnp.where(visible, scores, FLOOR), axis=1, keepdims=True)
    top = jnp.maximum(top_cache, top_draft)
    weights = jnp.where(visible, jnp.exp(scores - top), 0.0)
    scale = jnp.exp(top_cache - top)
    total = scale * total + jnp.sum(weights, axis=1, keepdims=True)
    summed = scale * summed + nn_dot(pltpu.roll(weights, 1, 1).astype(bf16), drafts)
    attn = (summed / total).astype(bf16)
    for i in range(PEERS):
        out_ref[i] = attn


def project_kernel(token_ref, own_ref, oth_ref, w_ref, stream_ref, out_ref, by_token):
    tp = lax.axis_index("tp")
    acc = jnp.zeros((TOKS, COLS), f32)
    for i in range(HEADS // 2):
        lhs = jnp.concatenate(
            [
                jnp.concatenate([own_ref[2 * i], own_ref[2 * i + 1]], axis=1),
                jnp.concatenate([oth_ref[2 * i], oth_ref[2 * i + 1]], axis=1),
            ],
            axis=0,
        )
        acc = acc + nn_dot(lhs, w_ref[2 * i * HD : (2 * i + 2) * HD, :])
    place = (row_ids((TOKS, HD)) == token_ref[0:1, :]).astype(bf16)[:, :TOKS]
    high = acc.astype(bf16)
    rest = acc - high.astype(f32)
    middle = rest.astype(bf16)
    low = (rest - middle.astype(f32)).astype(bf16)
    by_token[...] = nn_dot(place, high) + (nn_dot(place, middle) + nn_dot(place, low))
    mine = pl.ds(pl.multiple_of(tp * 16, 16), 16)
    by_token[mine, :] = by_token[mine, :] + stream_ref[...].astype(f32)
    for y in range(NY):
        rows = by_token[16 * y : 16 * y + 16, :].astype(bf16)
        for z in range(NZ):
            out_ref[z * NY + y] = rows


def spread_kernel(in_ref, gain_ref, out_ref, mid_ref, whole):
    mine = lax.axis_index("kvp") // NC
    x = lax.rem(mine, NX)
    for z in range(NZ):
        parts = [in_ref[z * NY + y].astype(f32) for y in range(NY)]
        middle = (parts[0] + parts[1]) + (parts[2] + parts[3])
        whole[z] = middle
        scaled = (middle * gain_ref[pl.ds(z * NX + x, 1), :]).astype(bf16)
        for i in range(NX * NY):
            out_ref[i, z * 16 : (z + 1) * 16, :] = scaled
    mid_ref[...] = whole[mine // NX]


def token_rows(src_ref, i):
    z, x = i // NX, i % NX
    return jnp.concatenate(
        [src_ref[x * NY + y, z * 16 : (z + 1) * 16, :] for y in range(NY)], axis=0
    )


def gate_kernel(rows_ref, gain_ref, gu_ref, gu2_ref, sums_ref):
    core = lax.rem(lax.axis_index("kvp"), 2)
    sums = [jnp.zeros((TOKS, 2 * HIDDEN), f32) for _ in range(2)]
    squares = jnp.zeros((TOKS, COLS), f32)
    inverse = 1.0 / gain_ref[...]
    for i in range(PEERS):
        rows = token_rows(rows_ref, i)
        middle = rows.astype(f32) * inverse[i : i + 1, :]
        squares = squares + middle * middle
        cols = pl.ds(pl.multiple_of((2 * i + core) * COLS, COLS), COLS)
        for j, ref in enumerate((gu_ref, gu2_ref)):
            both = jnp.concatenate([ref[0, :, cols], ref[1, :, cols]], axis=0)
            sums[j] = sums[j] + nt_dot(rows, both)
    for j in range(2):
        sums_ref[j, :, : 2 * HIDDEN] = sums[j]
    sums_ref[2] = jnp.broadcast_to(jnp.sum(squares, axis=1, keepdims=True), (TOKS, COLS))


def down_kernel(own_ref, oth_ref, down_ref, down2_ref, out_ref):
    core = lax.rem(lax.axis_index("kvp"), 2)
    squares = own_ref[2][:, 0:1] + oth_ref[2][:, 0:1]
    rscale = lax.rsqrt(squares / D + EPS)
    hidden = []
    for j in range(2):
        total = (own_ref[j] + oth_ref[1 - j]) * rscale
        gate, up = total[:, :HIDDEN], total[:, HIDDEN : 2 * HIDDEN]
        hidden.append((gate / (1.0 + jnp.exp(-gate)) * up).astype(bf16))
    for i in range(PEERS):
        z, x = i // NX, i % NX
        cols = pl.ds(pl.multiple_of((2 * i + core) * COLS, COLS), COLS)
        part = nn_dot(hidden[0], down_ref[:, cols]) + nn_dot(hidden[1], down2_ref[:, cols])
        part = part.astype(bf16)
        for y in range(NY):
            line = jnp.where(core == 0, x, y)
            rest = (x + y - line) * NZ + z
            out_ref[line, pl.ds(pl.multiple_of(rest * 16, 16), 16), :] = part[
                16 * y : 16 * y + 16
            ]


VMEM = pl.BlockSpec(memory_space=pltpu.VMEM)
SMEM = pl.BlockSpec(memory_space=pltpu.SMEM)
HBM = pl.BlockSpec(memory_space=pltpu.HBM)
COST = pl.CostEstimate(flops=10**9, bytes_accessed=4 * 10**7, transcendentals=0)
PARAMS = pltpu.CompilerParams(vmem_limit_bytes=VMEM_LIMIT)


def call(kernel, name, in_specs, out_shape, out_specs, scratch=(), cost=COST):
    return pl.pallas_call(
        kernel,
        name=name,
        in_specs=in_specs,
        out_shape=out_shape,
        out_specs=out_specs,
        scratch_shapes=list(scratch),
        compiler_params=PARAMS,
        cost_estimate=cost,
    )


def in_hbm(array):
    return pltpu.with_memory_space_constraint(array, pltpu.HBM)


def on_device(
    query,
    draft_kv,
    key_cache,
    value_cache,
    prompt_of,
    prefix_len,
    out_weight,
    stream,
    norm_gain,
    gate_up,
    down_weight,
):
    shape = jax.ShapeDtypeStruct
    cache = shape((PROMPTS // 2, SHARD, 2 * HD), bf16)
    key_pair, value_pair = swap_cores(key_cache), swap_cores(value_cache)
    draft_pair = swap_cores(draft_kv)
    block, keys, values, extra, order = call(
        prepare_kernel,
        "prepare",
        [SMEM, SMEM, VMEM, VMEM, VMEM, HBM, HBM],
        [
            shape((PEERS, HEADS, HD), bf16),
            cache,
            cache,
            shape((2, 8, HD), f32),
            shape((TOKS + PROMPTS,), jnp.int32),
        ],
        [VMEM, VMEM, VMEM, VMEM, SMEM],
        [
            pltpu.VMEM((HEADS, HD), f32),
            pltpu.SMEM((PROMPTS,), jnp.int32),
            pltpu.SemaphoreType.DMA((2,)),
        ],
        None,
    )(
        in_hbm(prompt_of),
        in_hbm(prefix_len),
        in_hbm(query),
        in_hbm(draft_kv),
        in_hbm(norm_gain),
        in_hbm(key_cache),
        in_hbm(value_cache),
    )
    block, draft_pair, key_pair, value_pair = lax.optimization_barrier(
        (block, draft_pair, key_pair, value_pair)
    )
    own = swap_plane(block)
    oth = swap_cores(own)
    part, queries, slot_token, row_token = call(
        attention_kernel,
        "attention",
        [SMEM] + [VMEM] * 8,
        [
            shape((HEADS, ROWS_OUT, HD), bf16),
            shape((HALF, HEADS, HD), bf16),
            shape((HALF, HD), jnp.int32),
            shape((8, HD), jnp.int32),
        ],
        [VMEM] * 4,
        [pltpu.VMEM((TOKS, HEADS, HD), bf16), pltpu.VMEM((8, HD), f32)],
    )(
        order,
        own,
        oth,
        keys,
        values,
        key_pair,
        value_pair,
        extra,
        draft_pair,
    )
    part, gate_up_sent = lax.optimization_barrier((part, gate_up))
    gate_up_pair = swap_cores(gate_up_sent)
    attn, gains = call(
        combine_kernel,
        "combine",
        [VMEM, VMEM, VMEM],
        [shape((PEERS, HALF, HD), bf16), shape((PEERS, COLS), f32)],
        [VMEM, VMEM],
        [pltpu.VMEM((PEERS, HD), f32), pltpu.VMEM((HD, HD), f32)],
    )(swap_plane(part), queries, slot_token)
    attn, down_sent = lax.optimization_barrier((attn, down_weight))
    down_pair = swap_cores(down_sent)
    attn_own = swap_plane(attn)
    attn_oth = swap_cores(attn_own)
    partial = call(
        project_kernel,
        "project",
        [VMEM] * 5,
        shape((NZ * NY, 16, COLS), bf16),
        VMEM,
        [pltpu.VMEM((TOKS, COLS), f32)],
    )(row_token, attn_own, attn_oth, out_weight, in_hbm(stream))
    partial = lax.all_to_all(partial, ("kvp", "tp"), 0, 0, axis_index_groups=G_YZ, tiled=True)
    msg, middle = call(
        spread_kernel,
        "spread",
        [VMEM, VMEM],
        [shape((NX * NY, NZ * 16, COLS), bf16), shape((16, COLS), f32)],
        [VMEM, VMEM],
        [pltpu.VMEM((NZ, 16, COLS), f32)],
    )(partial, gains)
    normed = swap_face(msg)
    sums = call(
        gate_kernel,
        "gate",
        [VMEM] * 4,
        shape((3, TOKS, COLS), f32),
        VMEM,
    )(normed, gains, gate_up, gate_up_pair)
    partial = call(
        down_kernel,
        "down",
        [VMEM] * 4,
        shape((4, 4 * NZ * 16, COLS), bf16),
        VMEM,
    )(sums, swap_cores(sums), down_weight, down_pair)
    summed = lax.all_to_all(partial, ("kvp", "tp"), 0, 0, axis_index_groups=G_LINE, tiled=True)
    summed = jnp.sum(summed.astype(f32), axis=0).astype(bf16).reshape(4 * NZ, 16, COLS)
    summed = lax.all_to_all(summed, ("kvp", "tp"), 0, 0, axis_index_groups=G_REST, tiled=True)
    return (middle + jnp.sum(summed.astype(f32), axis=0)).astype(bf16)


def solution(mesh):
    in_specs = (
        P("kvp", "tp"),
        P("kvp", None, "tp"),
        P(None, "kvp", "tp"),
        P(None, "kvp", "tp"),
        P(),
        P(),
        P("tp", "kvp"),
        P("tp", "kvp"),
        P("kvp"),
        P(None, ("kvp", "tp"), None),
        P(("kvp", "tp"), None),
    )
    out_specs = P("tp", "kvp")
    return jax.shard_map(
        on_device, mesh=mesh, in_specs=in_specs, out_specs=out_specs, check_vma=False
    )
```

```python
import jax
import jax.numpy as jnp
from jax import lax
from jax.experimental import pallas as pl
from jax.experimental.pallas import tpu as pltpu
from jax.sharding import PartitionSpec as P

D = 16384
HD = 128
NZ, NX, NC, NY = 8, 4, 2, 4
PEERS = NZ * NX
HEADS = 32
GROUP = 16
PROMPTS = 8
TOKS = 64
HALF = 32
SHARD = 128
COLS = 256
HIDDEN = 104
STAT_ROW = 4
GAIN_ROW = 5
ROWS_OUT = HALF + 8
EPS = 1e-05
SCALE = HD ** (-0.5)
FLOOR = -1e30
VMEM_LIMIT = 18 * 1024 * 1024

bf16 = jnp.bfloat16
f32 = jnp.float32


def kvp_index(z, x, c):
    return (z * NX + x) * NC + c


def all_index(z, x, c, y):
    return kvp_index(z, x, c) * NY + y


G_XZ = [[kvp_index(z, x, c) for z in range(NZ) for x in range(NX)] for c in range(NC)]
G_Z = [[kvp_index(z, x, c) for z in range(NZ)] for x in range(NX) for c in range(NC)]
G_XY = [
    [all_index(z, x, c, y) for x in range(NX) for y in range(NY)]
    for z in range(NZ)
    for c in range(NC)
]
G_YZ = [
    [all_index(z, x, c, y) for z in range(NZ) for y in range(NY)]
    for x in range(NX)
    for c in range(NC)
]
G_LINE = [[all_index(z, x, 0, y) for x in range(NX)] for z in range(NZ) for y in range(NY)] + [
    [all_index(z, x, 1, y) for y in range(NY)] for z in range(NZ) for x in range(NX)
]
G_REST = [[all_index(z, x, 0, y) for y in range(NY) for z in range(NZ)] for x in range(NX)] + [
    [all_index(z, x, 1, y) for x in range(NX) for z in range(NZ)] for y in range(NY)
]
CORE_PAIRS = [(i, i ^ 1) for i in range(NZ * NX * NC)]


def swap_cores(array):
    return lax.ppermute(array, "kvp", CORE_PAIRS)


def swap_plane(array):
    return lax.all_to_all(array, "kvp", 0, 0, axis_index_groups=G_XZ, tiled=True)


def swap_face(array):
    return lax.all_to_all(array, ("kvp", "tp"), 0, 0, axis_index_groups=G_XY, tiled=True)


def nt_dot(a, b):
    return lax.dot_general(a, b, (((1,), (1,)), ((), ())), preferred_element_type=f32)


def nn_dot(a, b):
    return jnp.dot(a, b, preferred_element_type=f32)


def lane_ids(shape):
    return lax.broadcasted_iota(jnp.int32, shape, len(shape) - 1)


def row_ids(shape):
    return lax.broadcasted_iota(jnp.int32, shape, len(shape) - 2)


def prepare_kernel(
    prompt_ref,
    len_ref,
    query_ref,
    draft_ref,
    gain_ref,
    k_ref,
    v_ref,
    block_ref,
    k_out,
    v_out,
    extra_ref,
    order_ref,
    rows,
    count,
    sems,
):
    half = pl.ds(lax.rem(lax.axis_index("kvp"), 2) * (PROMPTS // 2), PROMPTS // 2)
    k_copy = pltpu.make_async_copy(k_ref.at[half], k_out, sems.at[0])
    v_copy = pltpu.make_async_copy(v_ref.at[half], v_out, sems.at[1])
    k_copy.start()
    v_copy.start()
    query = query_ref[...].astype(f32)
    for h in range(HEADS):
        rows[h : h + 1, :] = query[:, h * HD : (h + 1) * HD]
    block = rows[...].astype(bf16)
    for i in range(PEERS):
        block_ref[i] = block
    extra_ref[...] = jnp.zeros((2, 8, HD), f32)
    gain = gain_ref[...].astype(f32).reshape(1, COLS)
    draft = draft_ref[0].astype(f32)
    for kv in range(2):
        for i in range(2):
            extra_ref[kv, i : i + 1, :] = draft[i : i + 1, kv * HD : (kv + 1) * HD]
            extra_ref[kv, GAIN_ROW + i : GAIN_ROW + i + 1, :] = gain[:, i * HD : (i + 1) * HD]
    for p in range(PROMPTS):
        count[p] = 0
        order_ref[TOKS + p] = len_ref[p]
    for s in range(HALF):
        p = prompt_ref[s]
        seen = jnp.minimum(count[p], 3)
        count[p] = seen + 1
        order_ref[p * 8 + seen] = s
        order_ref[p * 8 + 4 + seen] = s + HALF
    k_copy.wait()
    v_copy.wait()


def gather_row(order_ref, slot, core):
    t = order_ref[slot]
    return t // 2 + PEERS * lax.rem(t + core, 2)


def attention_kernel(
    order_ref,
    own_ref,
    oth_ref,
    k_ref,
    v_ref,
    k2_ref,
    v2_ref,
    extra_ref,
    draft2_ref,
    out_ref,
    query_ref,
    slot_ref,
    lane_ref,
    gath,
    tail,
):
    kvp = lax.axis_index("kvp")
    core = lax.rem(kvp, 2)
    gath[0:PEERS] = own_ref[...]
    gath[PEERS : 2 * PEERS] = oth_ref[...]
    to_row = row_ids((256, 256))
    from_row = lane_ids((256, 256))
    regroup = (
        (to_row // GROUP == from_row % GROUP) & (to_row % GROUP == from_row // GROUP)
    ).astype(bf16)
    by_group = (lane_ids((GROUP, SHARD)) % GROUP == row_ids((GROUP, SHARD))).astype(bf16)
    lanes = lane_ids((SHARD, SHARD))
    token = row_ids((SHARD, SHARD)) // GROUP
    here = kvp * SHARD + lanes
    there = (kvp + 1 - 2 * core) * SHARD + lanes
    position = jnp.concatenate([here, there], axis=1)
    slots = row_ids((HALF, HD))
    slot_token = jnp.zeros((HALF, HD), jnp.int32)
    for s in range(HALF):
        slot_token = jnp.where(slots == s, order_ref[HALF * core + s], slot_token)
    slot_ref[...] = slot_token
    row = lane_ids((8, HD))
    row_token = jnp.full((8, HD), -1, jnp.int32)
    for r in range(TOKS):
        row_token = jnp.where(row == r, order_ref[lax.rem(r + HALF * core, TOKS)], row_token)
    lane_ref[...] = row_token
    for kv in range(2):
        cols = slice(kv * HD, (kv + 1) * HD)
        stats = jnp.zeros((GROUP, SHARD), f32)
        for pair in range(2):
            parts = []
            for q_ in range(2):
                i = pair * 2 + q_
                p = i + 4 * core
                tiles = [
                    gath[gather_row(order_ref, p * 8 + j, core), kv * GROUP : (kv + 1) * GROUP, :]
                    for j in range(8)
                ]
                for j in range(8):
                    query_ref[i * 8 + j, kv * GROUP : (kv + 1) * GROUP, :] = tiles[j]
                queries = jnp.concatenate(tiles, axis=0)
                keys = jnp.concatenate([k_ref[i, :, cols], k2_ref[p, :, cols]], axis=0)
                values = jnp.concatenate([v_ref[i, :, cols], v2_ref[p, :, cols]], axis=0)
                scores = nt_dot(queries, keys) * SCALE
                visible = position < order_ref[TOKS + p]
                top = jnp.max(jnp.where(visible, scores, FLOOR), axis=1, keepdims=True)
                top = top.astype(bf16).astype(f32)
                weights = jnp.where(visible, jnp.exp(scores - top), 0.0)
                total = jnp.sum(weights, axis=1, keepdims=True)
                summed = nn_dot(weights.astype(bf16), values)
                parts.append(summed.astype(bf16))
                high = total.astype(bf16).astype(f32)
                low = total - high
                at = token + i * 8
                spread = jnp.where(
                    lanes == at,
                    top,
                    jnp.where(
                        lanes == at + HALF, high, jnp.where(lanes == at + 2 * HALF, low, 0.0)
                    ),
                )
                stats = stats + nn_dot(by_group, spread.astype(bf16))
            both = nn_dot(regroup, jnp.concatenate(parts, axis=0)).astype(bf16)
            for g in range(GROUP):
                out_ref[kv * GROUP + g, pair * 16 : pair * 16 + 16, :] = both[
                    g * 16 : (g + 1) * 16, :
                ]
        inner = row_ids((8, HD))
        tail[...] = extra_ref[kv]
        tail[2:4, :] = draft2_ref[0].astype(f32)[:, cols]
        extras = tail[...]
        for g in range(GROUP):
            out_ref[kv * GROUP + g, HALF:ROWS_OUT, :] = jnp.where(
                inner == STAT_ROW, stats[g : g + 1, :], extras
            ).astype(bf16)


def combine_kernel(part_ref, query_ref, slot_ref, out_ref, gain_ref, stat, turn):
    kvp = lax.axis_index("kvp")
    core = lax.rem(kvp, 2)
    head = kvp // 2
    kv = head // GROUP
    first = pl.multiple_of(kv * GROUP, GROUP)
    slot_token = slot_ref[...]
    query_tiles = [query_ref[s, pl.ds(first, GROUP), :] for s in range(HALF)]
    draft_tiles = []
    for i in range(PEERS):
        tile = part_ref[i, HALF:ROWS_OUT, :].astype(f32)
        draft_tiles.append(tile)
        stat[i : i + 1, :] = tile[STAT_ROW : STAT_ROW + 1, :]
        for j in range(2):
            gain_ref[i : i + 1, j * HD : (j + 1) * HD] = tile[GAIN_ROW + j : GAIN_ROW + j + 1, :]
    shape = (HALF, HALF * GROUP)
    pick = (
        (row_ids(shape) == lane_ids(shape) // GROUP) & (lane_ids(shape) % GROUP == head % GROUP)
    ).astype(bf16)
    queries = nn_dot(pick, jnp.concatenate(query_tiles, axis=0)).astype(bf16)
    drafts = jnp.concatenate(draft_tiles, axis=0).astype(bf16)
    scores = nt_dot(queries, drafts) * SCALE
    shape = (HALF, PEERS * 8)
    outer = lane_ids(shape) // 8
    inner = lane_ids(shape) % 8
    slot_token = jnp.concatenate([slot_token] * 2, axis=1)
    key_token = 2 * outer + jnp.where(inner == 0, core, 1 - core)
    visible = (
        ((inner == 0) | (inner == 2))
        & (slot_token % HALF == key_token % HALF)
        & (key_token // HALF <= slot_token // HALF)
    )
    stats = stat[...]
    top_row = jnp.max(stats, axis=0, keepdims=True)
    factors = jnp.exp(stats - top_row)
    totals = pltpu.roll(stats, HD - HALF, 1) + pltpu.roll(stats, HD - 2 * HALF, 1)
    turn[...] = jnp.zeros((HD, HD), f32)
    turn[0:PEERS, :] = factors
    turn[PEERS : PEERS + 1, :] = jnp.sum(factors * totals, axis=0, keepdims=True)
    turn[PEERS + 1 : PEERS + 2, :] = top_row
    turned = turn[...].T[0:HALF, :]
    total = turned[:, PEERS : PEERS + 1]
    top_cache = turned[:, PEERS + 1 : PEERS + 2]
    summed = jnp.zeros((HALF, HD), f32)
    for i in range(PEERS):
        summed = summed + turned[:, i : i + 1] * part_ref[i, 0:HALF, :].astype(f32)
    top_draft = jnp.max(jnp.where(visible, scores, FLOOR), axis=1, keepdims=True)
    top = jnp.maximum(top_cache, top_draft)
    weights = jnp.where(visible, jnp.exp(scores - top), 0.0)
    scale = jnp.exp(top_cache - top)
    total = scale * total + jnp.sum(weights, axis=1, keepdims=True)
    summed = scale * summed + nn_dot(pltpu.roll(weights, 1, 1).astype(bf16), drafts)
    attn = (summed / total).astype(bf16)
    for i in range(PEERS):
        out_ref[i] = attn


def project_kernel(token_ref, own_ref, oth_ref, w_ref, stream_ref, out_ref, by_token):
    tp = lax.axis_index("tp")
    acc = jnp.zeros((TOKS, COLS), f32)
    for i in range(HEADS // 2):
        lhs = jnp.concatenate(
            [
                jnp.concatenate([own_ref[2 * i], own_ref[2 * i + 1]], axis=1),
                jnp.concatenate([oth_ref[2 * i], oth_ref[2 * i + 1]], axis=1),
            ],
            axis=0,
        )
        acc = acc + nn_dot(lhs, w_ref[2 * i * HD : (2 * i + 2) * HD, :])
    place = (row_ids((TOKS, HD)) == token_ref[0:1, :]).astype(bf16)[:, :TOKS]
    high = acc.astype(bf16)
    rest = acc - high.astype(f32)
    middle = rest.astype(bf16)
    low = (rest - middle.astype(f32)).astype(bf16)
    split = nn_dot(place, jnp.concatenate([high, middle, low], axis=1))
    by_token[...] = split[:, :COLS] + (split[:, COLS : 2 * COLS] + split[:, 2 * COLS :])
    mine = pl.ds(pl.multiple_of(tp * 16, 16), 16)
    by_token[mine, :] = by_token[mine, :] + stream_ref[...].astype(f32)
    for y in range(NY):
        rows = by_token[16 * y : 16 * y + 16, :].astype(bf16)
        for z in range(NZ):
            out_ref[z * NY + y] = rows


def spread_kernel(in_ref, gain_ref, out_ref, mid_ref, whole):
    mine = lax.axis_index("kvp") // NC
    x = lax.rem(mine, NX)
    for z in range(NZ):
        parts = [in_ref[z * NY + y].astype(f32) for y in range(NY)]
        middle = (parts[0] + parts[1]) + (parts[2] + parts[3])
        whole[z] = middle
        scaled = (middle * gain_ref[pl.ds(z * NX + x, 1), :]).astype(bf16)
        for i in range(NX * NY):
            out_ref[i, z * 16 : (z + 1) * 16, :] = scaled
    mid_ref[...] = whole[mine // NX]


def token_rows(src_ref, i):
    z, x = i // NX, i % NX
    return jnp.concatenate(
        [src_ref[x * NY + y, z * 16 : (z + 1) * 16, :] for y in range(NY)], axis=0
    )


def gate_kernel(rows_ref, gain_ref, gu_ref, gu2_ref, sums_ref):
    core = lax.rem(lax.axis_index("kvp"), 2)
    sums = [jnp.zeros((TOKS, 2 * HIDDEN), f32) for _ in range(2)]
    squares = jnp.zeros((TOKS, COLS), f32)
    inverse = 1.0 / gain_ref[...]
    for i in range(PEERS):
        rows = token_rows(rows_ref, i)
        middle = rows.astype(f32) * inverse[i : i + 1, :]
        squares = squares + middle * middle
        cols = pl.ds(pl.multiple_of((2 * i + core) * COLS, COLS), COLS)
        for j, ref in enumerate((gu_ref, gu2_ref)):
            both = jnp.concatenate([ref[0, :, cols], ref[1, :, cols]], axis=0)
            sums[j] = sums[j] + nt_dot(rows, both)
    for j in range(2):
        sums_ref[j, :, : 2 * HIDDEN] = sums[j]
    sums_ref[2] = jnp.broadcast_to(jnp.sum(squares, axis=1, keepdims=True), (TOKS, COLS))


def down_kernel(own_ref, oth_ref, down_ref, down2_ref, out_ref):
    core = lax.rem(lax.axis_index("kvp"), 2)
    squares = own_ref[2][:, 0:1] + oth_ref[2][:, 0:1]
    rscale = lax.rsqrt(squares / D + EPS)
    hidden = []
    for j in range(2):
        total = (own_ref[j] + oth_ref[1 - j]) * rscale
        gate, up = total[:, :HIDDEN], total[:, HIDDEN : 2 * HIDDEN]
        hidden.append((gate / (1.0 + jnp.exp(-gate)) * up).astype(bf16))
    for i in range(PEERS):
        z, x = i // NX, i % NX
        cols = pl.ds(pl.multiple_of((2 * i + core) * COLS, COLS), COLS)
        part = nn_dot(hidden[0], down_ref[:, cols]) + nn_dot(hidden[1], down2_ref[:, cols])
        part = part.astype(bf16)
        for y in range(NY):
            line = jnp.where(core == 0, x, y)
            rest = (x + y - line) * NZ + z
            out_ref[line, pl.ds(pl.multiple_of(rest * 16, 16), 16), :] = part[
                16 * y : 16 * y + 16
            ]


def finish_kernel(parts_ref, middle_ref, out_ref):
    total = middle_ref[...]
    for i in range(4 * NZ):
        total = total + parts_ref[i].astype(f32)
    out_ref[...] = total.astype(bf16)


VMEM = pl.BlockSpec(memory_space=pltpu.VMEM)
SMEM = pl.BlockSpec(memory_space=pltpu.SMEM)
HBM = pl.BlockSpec(memory_space=pltpu.HBM)
COST = pl.CostEstimate(flops=10**9, bytes_accessed=4 * 10**7, transcendentals=0)
PARAMS = pltpu.CompilerParams(vmem_limit_bytes=VMEM_LIMIT)


def call(kernel, name, in_specs, out_shape, out_specs, scratch=(), cost=COST):
    return pl.pallas_call(
        kernel,
        name=name,
        in_specs=in_specs,
        out_shape=out_shape,
        out_specs=out_specs,
        scratch_shapes=list(scratch),
        compiler_params=PARAMS,
        cost_estimate=cost,
    )


def in_hbm(array):
    return pltpu.with_memory_space_constraint(array, pltpu.HBM)


def on_device(
    query,
    draft_kv,
    key_cache,
    value_cache,
    prompt_of,
    prefix_len,
    out_weight,
    stream,
    norm_gain,
    gate_up,
    down_weight,
):
    shape = jax.ShapeDtypeStruct
    cache = shape((PROMPTS // 2, SHARD, 2 * HD), bf16)
    key_pair, value_pair = swap_cores(key_cache), swap_cores(value_cache)
    draft_pair = swap_cores(draft_kv)
    block, keys, values, extra, order = call(
        prepare_kernel,
        "prepare",
        [SMEM, SMEM, VMEM, VMEM, VMEM, HBM, HBM],
        [
            shape((PEERS, HEADS, HD), bf16),
            cache,
            cache,
            shape((2, 8, HD), f32),
            shape((TOKS + PROMPTS,), jnp.int32),
        ],
        [VMEM, VMEM, VMEM, VMEM, SMEM],
        [
            pltpu.VMEM((HEADS, HD), f32),
            pltpu.SMEM((PROMPTS,), jnp.int32),
            pltpu.SemaphoreType.DMA((2,)),
        ],
        None,
    )(
        in_hbm(prompt_of),
        in_hbm(prefix_len),
        in_hbm(query),
        in_hbm(draft_kv),
        in_hbm(norm_gain),
        in_hbm(key_cache),
        in_hbm(value_cache),
    )
    block, draft_pair, key_pair, value_pair = lax.optimization_barrier(
        (block, draft_pair, key_pair, value_pair)
    )
    own = swap_plane(block)
    oth = swap_cores(own)
    part, queries, slot_token, row_token = call(
        attention_kernel,
        "attention",
        [SMEM] + [VMEM] * 8,
        [
            shape((HEADS, ROWS_OUT, HD), bf16),
            shape((HALF, HEADS, HD), bf16),
            shape((HALF, HD), jnp.int32),
            shape((8, HD), jnp.int32),
        ],
        [VMEM] * 4,
        [pltpu.VMEM((TOKS, HEADS, HD), bf16), pltpu.VMEM((8, HD), f32)],
    )(
        order,
        own,
        oth,
        keys,
        values,
        key_pair,
        value_pair,
        extra,
        draft_pair,
    )
    part, gate_up_sent = lax.optimization_barrier((part, gate_up))
    gate_up_pair = swap_cores(gate_up_sent)
    attn, gains = call(
        combine_kernel,
        "combine",
        [VMEM, VMEM, VMEM],
        [shape((PEERS, HALF, HD), bf16), shape((PEERS, COLS), f32)],
        [VMEM, VMEM],
        [pltpu.VMEM((PEERS, HD), f32), pltpu.VMEM((HD, HD), f32)],
    )(swap_plane(part), queries, slot_token)
    attn, down_sent = lax.optimization_barrier((attn, down_weight))
    down_pair = swap_cores(down_sent)
    attn_own = swap_plane(attn)
    attn_oth = swap_cores(attn_own)
    partial = call(
        project_kernel,
        "project",
        [VMEM] * 5,
        shape((NZ * NY, 16, COLS), bf16),
        VMEM,
        [pltpu.VMEM((TOKS, COLS), f32)],
    )(row_token, attn_own, attn_oth, out_weight, stream)
    partial = lax.all_to_all(partial, ("kvp", "tp"), 0, 0, axis_index_groups=G_YZ, tiled=True)
    msg, middle = call(
        spread_kernel,
        "spread",
        [VMEM, VMEM],
        [shape((NX * NY, NZ * 16, COLS), bf16), shape((16, COLS), f32)],
        [VMEM, VMEM],
        [pltpu.VMEM((NZ, 16, COLS), f32)],
    )(partial, gains)
    normed = swap_face(msg)
    sums = call(
        gate_kernel,
        "gate",
        [VMEM] * 4,
        shape((3, TOKS, COLS), f32),
        VMEM,
    )(normed, gains, gate_up, gate_up_pair)
    partial = call(
        down_kernel,
        "down",
        [VMEM] * 4,
        shape((4, 4 * NZ * 16, COLS), bf16),
        VMEM,
    )(sums, swap_cores(sums), down_weight, down_pair)
    summed = lax.all_to_all(partial, ("kvp", "tp"), 0, 0, axis_index_groups=G_LINE, tiled=True)
    summed = jnp.sum(summed.astype(f32), axis=0).astype(bf16).reshape(4 * NZ, 16, COLS)
    summed = lax.all_to_all(summed, ("kvp", "tp"), 0, 0, axis_index_groups=G_REST, tiled=True)
    return call(finish_kernel, "finish", [VMEM, VMEM], shape((16, COLS), bf16), VMEM)(
        summed, middle
    )


def solution(mesh):
    in_specs = (
        P("kvp", "tp"),
        P("kvp", None, "tp"),
        P(None, "kvp", "tp"),
        P(None, "kvp", "tp"),
        P(),
        P(),
        P("tp", "kvp"),
        P("tp", "kvp"),
        P("kvp"),
        P(None, ("kvp", "tp"), None),
        P(("kvp", "tp"), None),
    )
    out_specs = P("tp", "kvp")
    return jax.shard_map(
        on_device, mesh=mesh, in_specs=in_specs, out_specs=out_specs, check_vma=False
    )
```

```python
import jax
import jax.numpy as jnp
from jax import lax
from jax.experimental import pallas as pl
from jax.experimental.pallas import tpu as pltpu
from jax.sharding import PartitionSpec as P

D = 16384
HD = 128
NZ, NX, NC, NY = 8, 4, 2, 4
PEERS = NZ * NX
HEADS = 32
GROUP = 16
PROMPTS = 8
TOKS = 64
HALF = 32
SHARD = 128
COLS = 256
HIDDEN = 104
STAT_ROW = 4
GAIN_ROW = 5
ROWS_OUT = HALF + 8
EPS = 1e-05
SCALE = HD ** (-0.5)
FLOOR = -1e30
VMEM_LIMIT = 18 * 1024 * 1024

bf16 = jnp.bfloat16
f32 = jnp.float32


def kvp_index(z, x, c):
    return (z * NX + x) * NC + c


def all_index(z, x, c, y):
    return kvp_index(z, x, c) * NY + y


G_XZ = [[kvp_index(z, x, c) for z in range(NZ) for x in range(NX)] for c in range(NC)]
G_Z = [[kvp_index(z, x, c) for z in range(NZ)] for x in range(NX) for c in range(NC)]
G_XY = [
    [all_index(z, x, c, y) for x in range(NX) for y in range(NY)]
    for z in range(NZ)
    for c in range(NC)
]
G_YZ = [
    [all_index(z, x, c, y) for z in range(NZ) for y in range(NY)]
    for x in range(NX)
    for c in range(NC)
]
G_LINE = [[all_index(z, x, 0, y) for x in range(NX)] for z in range(NZ) for y in range(NY)] + [
    [all_index(z, x, 1, y) for y in range(NY)] for z in range(NZ) for x in range(NX)
]
G_REST = [[all_index(z, x, 0, y) for y in range(NY) for z in range(NZ)] for x in range(NX)] + [
    [all_index(z, x, 1, y) for x in range(NX) for z in range(NZ)] for y in range(NY)
]
CORE_PAIRS = [(i, i ^ 1) for i in range(NZ * NX * NC)]


def swap_cores(array):
    return lax.ppermute(array, "kvp", CORE_PAIRS)


def swap_plane(array):
    return lax.all_to_all(array, "kvp", 0, 0, axis_index_groups=G_XZ, tiled=True)


def swap_face(array):
    return lax.all_to_all(array, ("kvp", "tp"), 0, 0, axis_index_groups=G_XY, tiled=True)


def nt_dot(a, b):
    return lax.dot_general(a, b, (((1,), (1,)), ((), ())), preferred_element_type=f32)


def nn_dot(a, b):
    return jnp.dot(a, b, preferred_element_type=f32)


def lane_ids(shape):
    return lax.broadcasted_iota(jnp.int32, shape, len(shape) - 1)


def row_ids(shape):
    return lax.broadcasted_iota(jnp.int32, shape, len(shape) - 2)


def prepare_kernel(
    prompt_hbm,
    len_hbm,
    query_hbm,
    draft_hbm,
    gain_hbm,
    k_ref,
    v_ref,
    block_ref,
    k_out,
    v_out,
    extra_ref,
    order_ref,
    rows,
    count,
    prompt_ref,
    len_ref,
    query_ref,
    draft_ref,
    gain_ref,
    sems,
):
    half = pl.ds(lax.rem(lax.axis_index("kvp"), 2) * (PROMPTS // 2), PROMPTS // 2)
    pairs = (
        (prompt_hbm, prompt_ref),
        (len_hbm, len_ref),
        (query_hbm, query_ref),
        (draft_hbm, draft_ref),
        (gain_hbm, gain_ref),
        (k_ref.at[half], k_out),
        (v_ref.at[half], v_out),
    )
    copies = [pltpu.make_async_copy(*pair, sems.at[i]) for i, pair in enumerate(pairs)]
    for copy in copies:
        copy.start()
    for copy in copies[:5]:
        copy.wait()
    query = query_ref[...].astype(f32)
    for h in range(HEADS):
        rows[h : h + 1, :] = query[:, h * HD : (h + 1) * HD]
    block = rows[...].astype(bf16)
    for i in range(PEERS):
        block_ref[i] = block
    extra_ref[...] = jnp.zeros((2, 8, HD), f32)
    gain = gain_ref[...].astype(f32).reshape(1, COLS)
    draft = draft_ref[0].astype(f32)
    for kv in range(2):
        for i in range(2):
            extra_ref[kv, i : i + 1, :] = draft[i : i + 1, kv * HD : (kv + 1) * HD]
            extra_ref[kv, GAIN_ROW + i : GAIN_ROW + i + 1, :] = gain[:, i * HD : (i + 1) * HD]
    for p in range(PROMPTS):
        count[p] = 0
        order_ref[TOKS + p] = len_ref[p]
    for s in range(HALF):
        p = prompt_ref[s]
        seen = jnp.minimum(count[p], 3)
        count[p] = seen + 1
        order_ref[p * 8 + seen] = s
        order_ref[p * 8 + 4 + seen] = s + HALF
    for copy in copies[5:]:
        copy.wait()


def gather_row(order_ref, slot, core):
    t = order_ref[slot]
    return t // 2 + PEERS * lax.rem(t + core, 2)


def attention_kernel(
    order_ref,
    own_ref,
    oth_ref,
    k_ref,
    v_ref,
    k2_ref,
    v2_ref,
    extra_ref,
    draft2_ref,
    out_ref,
    query_ref,
    slot_ref,
    lane_ref,
    gath,
    tail,
):
    kvp = lax.axis_index("kvp")
    core = lax.rem(kvp, 2)
    gath[0:PEERS] = own_ref[...]
    gath[PEERS : 2 * PEERS] = oth_ref[...]
    to_row = row_ids((256, 256))
    from_row = lane_ids((256, 256))
    regroup = (
        (to_row // GROUP == from_row % GROUP) & (to_row % GROUP == from_row // GROUP)
    ).astype(bf16)
    by_group = (lane_ids((GROUP, SHARD)) % GROUP == row_ids((GROUP, SHARD))).astype(bf16)
    lanes = lane_ids((SHARD, SHARD))
    token = row_ids((SHARD, SHARD)) // GROUP
    here = kvp * SHARD + lanes
    there = (kvp + 1 - 2 * core) * SHARD + lanes
    position = jnp.concatenate([here, there], axis=1)
    slots = row_ids((HALF, HD))
    slot_token = jnp.zeros((HALF, HD), jnp.int32)
    for s in range(HALF):
        slot_token = jnp.where(slots == s, order_ref[HALF * core + s], slot_token)
    slot_ref[...] = slot_token
    row = lane_ids((8, HD))
    row_token = jnp.full((8, HD), -1, jnp.int32)
    for r in range(TOKS):
        row_token = jnp.where(row == r, order_ref[lax.rem(r + HALF * core, TOKS)], row_token)
    lane_ref[...] = row_token
    for kv in range(2):
        cols = slice(kv * HD, (kv + 1) * HD)
        stats = jnp.zeros((GROUP, SHARD), f32)
        for pair in range(2):
            parts = []
            for q_ in range(2):
                i = pair * 2 + q_
                p = i + 4 * core
                tiles = [
                    gath[gather_row(order_ref, p * 8 + j, core), kv * GROUP : (kv + 1) * GROUP, :]
                    for j in range(8)
                ]
                for j in range(8):
                    query_ref[i * 8 + j, kv * GROUP : (kv + 1) * GROUP, :] = tiles[j]
                queries = jnp.concatenate(tiles, axis=0)
                keys = jnp.concatenate([k_ref[i, :, cols], k2_ref[p, :, cols]], axis=0)
                values = jnp.concatenate([v_ref[i, :, cols], v2_ref[p, :, cols]], axis=0)
                scores = nt_dot(queries, keys) * SCALE
                visible = position < order_ref[TOKS + p]
                top = jnp.max(jnp.where(visible, scores, FLOOR), axis=1, keepdims=True)
                top = top.astype(bf16).astype(f32)
                weights = jnp.where(visible, jnp.exp(scores - top), 0.0)
                total = jnp.sum(weights, axis=1, keepdims=True)
                summed = nn_dot(weights.astype(bf16), values)
                parts.append(summed.astype(bf16))
                high = total.astype(bf16).astype(f32)
                low = total - high
                at = token + i * 8
                spread = jnp.where(
                    lanes == at,
                    top,
                    jnp.where(
                        lanes == at + HALF, high, jnp.where(lanes == at + 2 * HALF, low, 0.0)
                    ),
                )
                stats = stats + nn_dot(by_group, spread.astype(bf16))
            both = nn_dot(regroup, jnp.concatenate(parts, axis=0)).astype(bf16)
            for g in range(GROUP):
                out_ref[kv * GROUP + g, pair * 16 : pair * 16 + 16, :] = both[
                    g * 16 : (g + 1) * 16, :
                ]
        inner = row_ids((8, HD))
        tail[...] = extra_ref[kv]
        tail[2:4, :] = draft2_ref[0].astype(f32)[:, cols]
        extras = tail[...]
        for g in range(GROUP):
            out_ref[kv * GROUP + g, HALF:ROWS_OUT, :] = jnp.where(
                inner == STAT_ROW, stats[g : g + 1, :], extras
            ).astype(bf16)


def combine_kernel(part_ref, query_ref, slot_ref, out_ref, gain_ref, stat, turn):
    kvp = lax.axis_index("kvp")
    core = lax.rem(kvp, 2)
    head = kvp // 2
    kv = head // GROUP
    first = pl.multiple_of(kv * GROUP, GROUP)
    slot_token = slot_ref[...]
    query_tiles = [query_ref[s, pl.ds(first, GROUP), :] for s in range(HALF)]
    draft_tiles = []
    for i in range(PEERS):
        tile = part_ref[i, HALF:ROWS_OUT, :].astype(f32)
        draft_tiles.append(tile)
        stat[i : i + 1, :] = tile[STAT_ROW : STAT_ROW + 1, :]
        for j in range(2):
            gain_ref[i : i + 1, j * HD : (j + 1) * HD] = tile[GAIN_ROW + j : GAIN_ROW + j + 1, :]
    shape = (HALF, HALF * GROUP)
    pick = (
        (row_ids(shape) == lane_ids(shape) // GROUP) & (lane_ids(shape) % GROUP == head % GROUP)
    ).astype(bf16)
    queries = nn_dot(pick, jnp.concatenate(query_tiles, axis=0)).astype(bf16)
    drafts = jnp.concatenate(draft_tiles, axis=0).astype(bf16)
    scores = nt_dot(queries, drafts) * SCALE
    shape = (HALF, PEERS * 8)
    outer = lane_ids(shape) // 8
    inner = lane_ids(shape) % 8
    slot_token = jnp.concatenate([slot_token] * 2, axis=1)
    key_token = 2 * outer + jnp.where(inner == 0, core, 1 - core)
    visible = (
        ((inner == 0) | (inner == 2))
        & (slot_token % HALF == key_token % HALF)
        & (key_token // HALF <= slot_token // HALF)
    )
    stats = stat[...]
    top_row = jnp.max(stats, axis=0, keepdims=True)
    factors = jnp.exp(stats - top_row)
    totals = pltpu.roll(stats, HD - HALF, 1) + pltpu.roll(stats, HD - 2 * HALF, 1)
    turn[...] = jnp.zeros((HD, HD), f32)
    turn[0:PEERS, :] = factors
    turn[PEERS : PEERS + 1, :] = jnp.sum(factors * totals, axis=0, keepdims=True)
    turn[PEERS + 1 : PEERS + 2, :] = top_row
    turned = turn[...].T[0:HALF, :]
    total = turned[:, PEERS : PEERS + 1]
    top_cache = turned[:, PEERS + 1 : PEERS + 2]
    summed = jnp.zeros((HALF, HD), f32)
    for i in range(PEERS):
        summed = summed + turned[:, i : i + 1] * part_ref[i, 0:HALF, :].astype(f32)
    top_draft = jnp.max(jnp.where(visible, scores, FLOOR), axis=1, keepdims=True)
    top = jnp.maximum(top_cache, top_draft)
    weights = jnp.where(visible, jnp.exp(scores - top), 0.0)
    scale = jnp.exp(top_cache - top)
    total = scale * total + jnp.sum(weights, axis=1, keepdims=True)
    summed = scale * summed + nn_dot(pltpu.roll(weights, 1, 1).astype(bf16), drafts)
    attn = (summed / total).astype(bf16)
    for i in range(PEERS):
        out_ref[i] = attn


def project_kernel(token_ref, own_ref, oth_ref, w_ref, stream_ref, out_ref, by_token):
    tp = lax.axis_index("tp")
    acc = jnp.zeros((TOKS, COLS), f32)
    for i in range(HEADS // 2):
        lhs = jnp.concatenate(
            [
                jnp.concatenate([own_ref[2 * i], own_ref[2 * i + 1]], axis=1),
                jnp.concatenate([oth_ref[2 * i], oth_ref[2 * i + 1]], axis=1),
            ],
            axis=0,
        )
        acc = acc + nn_dot(lhs, w_ref[2 * i * HD : (2 * i + 2) * HD, :])
    place = (row_ids((TOKS, HD)) == token_ref[0:1, :]).astype(bf16)[:, :TOKS]
    high = acc.astype(bf16)
    rest = acc - high.astype(f32)
    middle = rest.astype(bf16)
    low = (rest - middle.astype(f32)).astype(bf16)
    split = nn_dot(place, jnp.concatenate([high, middle, low], axis=1))
    by_token[...] = split[:, :COLS] + (split[:, COLS : 2 * COLS] + split[:, 2 * COLS :])
    mine = pl.ds(pl.multiple_of(tp * 16, 16), 16)
    by_token[mine, :] = by_token[mine, :] + stream_ref[...].astype(f32)
    for y in range(NY):
        rows = by_token[16 * y : 16 * y + 16, :].astype(bf16)
        for z in range(NZ):
            out_ref[z * NY + y] = rows


def spread_kernel(in_ref, gain_ref, out_ref, mid_ref, whole):
    mine = lax.axis_index("kvp") // NC
    x = lax.rem(mine, NX)
    for z in range(NZ):
        parts = [in_ref[z * NY + y].astype(f32) for y in range(NY)]
        middle = (parts[0] + parts[1]) + (parts[2] + parts[3])
        whole[z] = middle
        scaled = (middle * gain_ref[pl.ds(z * NX + x, 1), :]).astype(bf16)
        for i in range(NX * NY):
            out_ref[i, z * 16 : (z + 1) * 16, :] = scaled
    mid_ref[...] = whole[mine // NX]


def token_rows(src_ref, i):
    z, x = i // NX, i % NX
    return jnp.concatenate(
        [src_ref[x * NY + y, z * 16 : (z + 1) * 16, :] for y in range(NY)], axis=0
    )


def gate_kernel(rows_ref, gain_ref, gu_ref, gu2_ref, sums_ref):
    core = lax.rem(lax.axis_index("kvp"), 2)
    sums = [jnp.zeros((TOKS, 2 * HIDDEN), f32) for _ in range(2)]
    squares = jnp.zeros((TOKS, COLS), f32)
    inverse = 1.0 / gain_ref[...]
    for i in range(PEERS):
        rows = token_rows(rows_ref, i)
        middle = rows.astype(f32) * inverse[i : i + 1, :]
        squares = squares + middle * middle
        cols = pl.ds(pl.multiple_of((2 * i + core) * COLS, COLS), COLS)
        for j, ref in enumerate((gu_ref, gu2_ref)):
            both = jnp.concatenate([ref[0, :, cols], ref[1, :, cols]], axis=0)
            sums[j] = sums[j] + nt_dot(rows, both)
    for j in range(2):
        sums_ref[j, :, : 2 * HIDDEN] = sums[j]
    sums_ref[2] = jnp.broadcast_to(jnp.sum(squares, axis=1, keepdims=True), (TOKS, COLS))


def down_kernel(own_ref, oth_ref, down_ref, down2_ref, out_ref):
    core = lax.rem(lax.axis_index("kvp"), 2)
    squares = own_ref[2][:, 0:1] + oth_ref[2][:, 0:1]
    rscale = lax.rsqrt(squares / D + EPS)
    hidden = []
    for j in range(2):
        total = (own_ref[j] + oth_ref[1 - j]) * rscale
        gate, up = total[:, :HIDDEN], total[:, HIDDEN : 2 * HIDDEN]
        hidden.append((gate / (1.0 + jnp.exp(-gate)) * up).astype(bf16))
    for i in range(PEERS):
        z, x = i // NX, i % NX
        cols = pl.ds(pl.multiple_of((2 * i + core) * COLS, COLS), COLS)
        part = nn_dot(hidden[0], down_ref[:, cols]) + nn_dot(hidden[1], down2_ref[:, cols])
        part = part.astype(bf16)
        for y in range(NY):
            line = jnp.where(core == 0, x, y)
            rest = (x + y - line) * NZ + z
            out_ref[line, pl.ds(pl.multiple_of(rest * 16, 16), 16), :] = part[
                16 * y : 16 * y + 16
            ]


def finish_kernel(parts_ref, middle_ref, out_ref):
    total = middle_ref[...]
    for i in range(4 * NZ):
        total = total + parts_ref[i].astype(f32)
    out_ref[...] = total.astype(bf16)


VMEM = pl.BlockSpec(memory_space=pltpu.VMEM)
SMEM = pl.BlockSpec(memory_space=pltpu.SMEM)
HBM = pl.BlockSpec(memory_space=pltpu.HBM)
COST = pl.CostEstimate(flops=10**9, bytes_accessed=4 * 10**7, transcendentals=0)
PARAMS = pltpu.CompilerParams(vmem_limit_bytes=VMEM_LIMIT)


def call(kernel, name, in_specs, out_shape, out_specs, scratch=(), cost=COST):
    return pl.pallas_call(
        kernel,
        name=name,
        in_specs=in_specs,
        out_shape=out_shape,
        out_specs=out_specs,
        scratch_shapes=list(scratch),
        compiler_params=PARAMS,
        cost_estimate=cost,
    )


def in_hbm(array):
    return pltpu.with_memory_space_constraint(array, pltpu.HBM)


def on_device(
    query,
    draft_kv,
    key_cache,
    value_cache,
    prompt_of,
    prefix_len,
    out_weight,
    stream,
    norm_gain,
    gate_up,
    down_weight,
):
    shape = jax.ShapeDtypeStruct
    cache = shape((PROMPTS // 2, SHARD, 2 * HD), bf16)
    key_pair, value_pair = swap_cores(key_cache), swap_cores(value_cache)
    draft_pair = swap_cores(draft_kv)
    block, keys, values, extra, order = call(
        prepare_kernel,
        "prepare",
        [HBM] * 7,
        [
            shape((PEERS, HEADS, HD), bf16),
            cache,
            cache,
            shape((2, 8, HD), f32),
            shape((TOKS + PROMPTS,), jnp.int32),
        ],
        [VMEM, VMEM, VMEM, VMEM, SMEM],
        [
            pltpu.VMEM((HEADS, HD), f32),
            pltpu.SMEM((PROMPTS,), jnp.int32),
            pltpu.SMEM((HALF,), jnp.int32),
            pltpu.SMEM((PROMPTS,), jnp.int32),
            pltpu.VMEM((1, HEADS * HD), bf16),
            pltpu.VMEM((1, 2, 2 * HD), bf16),
            pltpu.VMEM((COLS,), bf16),
            pltpu.SemaphoreType.DMA((7,)),
        ],
        None,
    )(
        in_hbm(prompt_of),
        in_hbm(prefix_len),
        in_hbm(query),
        in_hbm(draft_kv),
        in_hbm(norm_gain),
        in_hbm(key_cache),
        in_hbm(value_cache),
    )
    block, draft_pair, key_pair, value_pair = lax.optimization_barrier(
        (block, draft_pair, key_pair, value_pair)
    )
    own = swap_plane(block)
    oth = swap_cores(own)
    part, queries, slot_token, row_token = call(
        attention_kernel,
        "attention",
        [SMEM] + [VMEM] * 8,
        [
            shape((HEADS, ROWS_OUT, HD), bf16),
            shape((HALF, HEADS, HD), bf16),
            shape((HALF, HD), jnp.int32),
            shape((8, HD), jnp.int32),
        ],
        [VMEM] * 4,
        [pltpu.VMEM((TOKS, HEADS, HD), bf16), pltpu.VMEM((8, HD), f32)],
    )(
        order,
        own,
        oth,
        keys,
        values,
        key_pair,
        value_pair,
        extra,
        draft_pair,
    )
    part, gate_up_sent = lax.optimization_barrier((part, gate_up))
    gate_up_pair = swap_cores(gate_up_sent)
    attn, gains = call(
        combine_kernel,
        "combine",
        [VMEM, VMEM, VMEM],
        [shape((PEERS, HALF, HD), bf16), shape((PEERS, COLS), f32)],
        [VMEM, VMEM],
        [pltpu.VMEM((PEERS, HD), f32), pltpu.VMEM((HD, HD), f32)],
    )(swap_plane(part), queries, slot_token)
    attn_own = swap_plane(attn)
    attn_oth = swap_cores(attn_own)
    attn_oth, down_sent = lax.optimization_barrier((attn_oth, down_weight))
    down_pair = swap_cores(down_sent)
    partial = call(
        project_kernel,
        "project",
        [VMEM] * 5,
        shape((NZ * NY, 16, COLS), bf16),
        VMEM,
        [pltpu.VMEM((TOKS, COLS), f32)],
    )(row_token, attn_own, attn_oth, out_weight, stream)
    partial = lax.all_to_all(partial, ("kvp", "tp"), 0, 0, axis_index_groups=G_YZ, tiled=True)
    msg, middle = call(
        spread_kernel,
        "spread",
        [VMEM, VMEM],
        [shape((NX * NY, NZ * 16, COLS), bf16), shape((16, COLS), f32)],
        [VMEM, VMEM],
        [pltpu.VMEM((NZ, 16, COLS), f32)],
    )(partial, gains)
    normed = swap_face(msg)
    sums = call(
        gate_kernel,
        "gate",
        [VMEM] * 4,
        shape((3, TOKS, COLS), f32),
        VMEM,
    )(normed, gains, gate_up, gate_up_pair)
    partial = call(
        down_kernel,
        "down",
        [VMEM] * 4,
        shape((4, 4 * NZ * 16, COLS), bf16),
        VMEM,
    )(sums, swap_cores(sums), down_weight, down_pair)
    summed = lax.all_to_all(partial, ("kvp", "tp"), 0, 0, axis_index_groups=G_LINE, tiled=True)
    summed = jnp.sum(summed.astype(f32), axis=0).astype(bf16).reshape(4 * NZ, 16, COLS)
    summed = lax.all_to_all(summed, ("kvp", "tp"), 0, 0, axis_index_groups=G_REST, tiled=True)
    return call(finish_kernel, "finish", [VMEM, VMEM], shape((16, COLS), bf16), VMEM)(
        summed, middle
    )


def solution(mesh):
    in_specs = (
        P("kvp", "tp"),
        P("kvp", None, "tp"),
        P(None, "kvp", "tp"),
        P(None, "kvp", "tp"),
        P(),
        P(),
        P("tp", "kvp"),
        P("tp", "kvp"),
        P("kvp"),
        P(None, ("kvp", "tp"), None),
        P(("kvp", "tp"), None),
    )
    out_specs = P("tp", "kvp")
    return jax.shard_map(
        on_device, mesh=mesh, in_specs=in_specs, out_specs=out_specs, check_vma=False
    )
```

```python
import jax
import jax.numpy as jnp
from jax import lax
from jax.experimental import pallas as pl
from jax.experimental.pallas import tpu as pltpu
from jax.sharding import PartitionSpec as P

D = 16384
HD = 128
NZ, NX, NC, NY = 8, 4, 2, 4
PEERS = NZ * NX
HEADS = 32
GROUP = 16
PROMPTS = 8
TOKS = 64
HALF = 32
SHARD = 128
COLS = 256
HIDDEN = 104
STAT_ROW = 4
GAIN_ROW = 5
ROWS_OUT = HALF + 8
EPS = 1e-05
SCALE = HD ** (-0.5)
FLOOR = -1e30
VMEM_LIMIT = 18 * 1024 * 1024

bf16 = jnp.bfloat16
f32 = jnp.float32


def kvp_index(z, x, c):
    return (z * NX + x) * NC + c


def all_index(z, x, c, y):
    return kvp_index(z, x, c) * NY + y


G_XZ = [[kvp_index(z, x, c) for z in range(NZ) for x in range(NX)] for c in range(NC)]
G_Z = [[kvp_index(z, x, c) for z in range(NZ)] for x in range(NX) for c in range(NC)]
G_XY = [
    [all_index(z, x, c, y) for x in range(NX) for y in range(NY)]
    for z in range(NZ)
    for c in range(NC)
]
G_YZ = [
    [all_index(z, x, c, y) for z in range(NZ) for y in range(NY)]
    for x in range(NX)
    for c in range(NC)
]
G_LINE = [[all_index(z, x, 0, y) for x in range(NX)] for z in range(NZ) for y in range(NY)] + [
    [all_index(z, x, 1, y) for y in range(NY)] for z in range(NZ) for x in range(NX)
]
G_REST = [[all_index(z, x, 0, y) for y in range(NY) for z in range(NZ)] for x in range(NX)] + [
    [all_index(z, x, 1, y) for x in range(NX) for z in range(NZ)] for y in range(NY)
]
CORE_PAIRS = [(i, i ^ 1) for i in range(NZ * NX * NC)]


def swap_cores(array):
    return lax.ppermute(array, "kvp", CORE_PAIRS)


def swap_plane(array):
    return lax.all_to_all(array, "kvp", 0, 0, axis_index_groups=G_XZ, tiled=True)


def swap_face(array):
    return lax.all_to_all(array, ("kvp", "tp"), 0, 0, axis_index_groups=G_XY, tiled=True)


def nt_dot(a, b):
    return lax.dot_general(a, b, (((1,), (1,)), ((), ())), preferred_element_type=f32)


def nn_dot(a, b):
    return jnp.dot(a, b, preferred_element_type=f32)


def lane_ids(shape):
    return lax.broadcasted_iota(jnp.int32, shape, len(shape) - 1)


def row_ids(shape):
    return lax.broadcasted_iota(jnp.int32, shape, len(shape) - 2)


def prepare_kernel(
    prompt_hbm,
    len_hbm,
    query_hbm,
    draft_hbm,
    gain_hbm,
    k_ref,
    v_ref,
    block_ref,
    k_out,
    v_out,
    extra_ref,
    order_ref,
    rows,
    count,
    prompt_ref,
    len_ref,
    query_ref,
    draft_ref,
    gain_ref,
    sems,
):
    half = pl.ds(lax.rem(lax.axis_index("kvp"), 2) * (PROMPTS // 2), PROMPTS // 2)
    pairs = (
        (prompt_hbm, prompt_ref),
        (len_hbm, len_ref),
        (query_hbm, query_ref),
        (draft_hbm, draft_ref),
        (gain_hbm, gain_ref),
        (k_ref.at[half], k_out),
        (v_ref.at[half], v_out),
    )
    copies = [pltpu.make_async_copy(*pair, sems.at[i]) for i, pair in enumerate(pairs)]
    for copy in copies:
        copy.start()
    for copy in copies[:5]:
        copy.wait()
    query = query_ref[...].astype(f32)
    for h in range(HEADS):
        rows[h : h + 1, :] = query[:, h * HD : (h + 1) * HD]
    block = rows[...].astype(bf16)
    for i in range(PEERS):
        block_ref[i] = block
    extra_ref[...] = jnp.zeros((2, 8, HD), f32)
    gain = gain_ref[...].astype(f32).reshape(1, COLS)
    draft = draft_ref[0].astype(f32)
    for kv in range(2):
        for i in range(2):
            extra_ref[kv, i : i + 1, :] = draft[i : i + 1, kv * HD : (kv + 1) * HD]
            extra_ref[kv, GAIN_ROW + i : GAIN_ROW + i + 1, :] = gain[:, i * HD : (i + 1) * HD]
    for p in range(PROMPTS):
        count[p] = 0
        order_ref[TOKS + p] = len_ref[p]
    for s in range(HALF):
        p = prompt_ref[s]
        seen = jnp.minimum(count[p], 3)
        count[p] = seen + 1
        order_ref[p * 8 + seen] = s
        order_ref[p * 8 + 4 + seen] = s + HALF
    for copy in copies[5:]:
        copy.wait()


def gather_row(order_ref, slot, core):
    t = order_ref[slot]
    return t // 2 + PEERS * lax.rem(t + core, 2)


def attention_kernel(
    order_ref,
    own_ref,
    oth_ref,
    k_ref,
    v_ref,
    k2_ref,
    v2_ref,
    extra_ref,
    draft2_ref,
    out_ref,
    query_ref,
    slot_ref,
    lane_ref,
    gath,
    tail,
):
    kvp = lax.axis_index("kvp")
    core = lax.rem(kvp, 2)
    gath[0:PEERS] = own_ref[...]
    gath[PEERS : 2 * PEERS] = oth_ref[...]
    to_row = row_ids((256, 256))
    from_row = lane_ids((256, 256))
    regroup = (
        (to_row // GROUP == from_row % GROUP) & (to_row % GROUP == from_row // GROUP)
    ).astype(bf16)
    by_group = (lane_ids((GROUP, SHARD)) % GROUP == row_ids((GROUP, SHARD))).astype(bf16)
    lanes = lane_ids((SHARD, SHARD))
    token = row_ids((SHARD, SHARD)) // GROUP
    here = kvp * SHARD + lanes
    there = (kvp + 1 - 2 * core) * SHARD + lanes
    position = jnp.concatenate([here, there], axis=1)
    slots = row_ids((HALF, HD))
    slot_token = jnp.zeros((HALF, HD), jnp.int32)
    for s in range(HALF):
        slot_token = jnp.where(slots == s, order_ref[HALF * core + s], slot_token)
    slot_ref[...] = slot_token
    row = lane_ids((8, HD))
    row_token = jnp.full((8, HD), -1, jnp.int32)
    for r in range(TOKS):
        row_token = jnp.where(row == r, order_ref[lax.rem(r + HALF * core, TOKS)], row_token)
    lane_ref[...] = row_token
    for kv in range(2):
        cols = slice(kv * HD, (kv + 1) * HD)
        stats = jnp.zeros((GROUP, SHARD), f32)
        for pair in range(2):
            parts = []
            for q_ in range(2):
                i = pair * 2 + q_
                p = i + 4 * core
                tiles = [
                    gath[gather_row(order_ref, p * 8 + j, core), kv * GROUP : (kv + 1) * GROUP, :]
                    for j in range(8)
                ]
                for j in range(8):
                    query_ref[i * 8 + j, kv * GROUP : (kv + 1) * GROUP, :] = tiles[j]
                queries = jnp.concatenate(tiles, axis=0)
                keys = jnp.concatenate([k_ref[i, :, cols], k2_ref[p, :, cols]], axis=0)
                values = jnp.concatenate([v_ref[i, :, cols], v2_ref[p, :, cols]], axis=0)
                scores = nt_dot(queries, keys) * SCALE
                visible = position < order_ref[TOKS + p]
                top = jnp.max(jnp.where(visible, scores, FLOOR), axis=1, keepdims=True)
                top = top.astype(bf16).astype(f32)
                weights = jnp.where(visible, jnp.exp(scores - top), 0.0)
                total = jnp.sum(weights, axis=1, keepdims=True)
                summed = nn_dot(weights.astype(bf16), values)
                parts.append(summed.astype(bf16))
                high = total.astype(bf16).astype(f32)
                low = total - high
                at = token + i * 8
                spread = jnp.where(
                    lanes == at,
                    top,
                    jnp.where(
                        lanes == at + HALF, high, jnp.where(lanes == at + 2 * HALF, low, 0.0)
                    ),
                )
                stats = stats + nn_dot(by_group, spread.astype(bf16))
            both = nn_dot(regroup, jnp.concatenate(parts, axis=0)).astype(bf16)
            for g in range(GROUP):
                out_ref[kv * GROUP + g, pair * 16 : pair * 16 + 16, :] = both[
                    g * 16 : (g + 1) * 16, :
                ]
        inner = row_ids((8, HD))
        tail[...] = extra_ref[kv]
        tail[2:4, :] = draft2_ref[0].astype(f32)[:, cols]
        extras = tail[...]
        for g in range(GROUP):
            out_ref[kv * GROUP + g, HALF:ROWS_OUT, :] = jnp.where(
                inner == STAT_ROW, stats[g : g + 1, :], extras
            ).astype(bf16)


def combine_kernel(part_ref, query_ref, slot_ref, out_ref, gain_ref, stat, turn):
    kvp = lax.axis_index("kvp")
    core = lax.rem(kvp, 2)
    head = kvp // 2
    kv = head // GROUP
    first = pl.multiple_of(kv * GROUP, GROUP)
    slot_token = slot_ref[...]
    query_tiles = [query_ref[s, pl.ds(first, GROUP), :] for s in range(HALF)]
    draft_tiles = []
    for i in range(PEERS):
        tile = part_ref[i, HALF:ROWS_OUT, :].astype(f32)
        draft_tiles.append(tile)
        stat[i : i + 1, :] = tile[STAT_ROW : STAT_ROW + 1, :]
        for j in range(2):
            gain_ref[i : i + 1, j * HD : (j + 1) * HD] = tile[GAIN_ROW + j : GAIN_ROW + j + 1, :]
    shape = (HALF, HALF * GROUP)
    pick = (
        (row_ids(shape) == lane_ids(shape) // GROUP) & (lane_ids(shape) % GROUP == head % GROUP)
    ).astype(bf16)
    queries = nn_dot(pick, jnp.concatenate(query_tiles, axis=0)).astype(bf16)
    drafts = jnp.concatenate(draft_tiles, axis=0).astype(bf16)
    scores = nt_dot(queries, drafts) * SCALE
    shape = (HALF, PEERS * 8)
    outer = lane_ids(shape) // 8
    inner = lane_ids(shape) % 8
    slot_token = jnp.concatenate([slot_token] * 2, axis=1)
    key_token = 2 * outer + jnp.where(inner == 0, core, 1 - core)
    visible = (
        ((inner == 0) | (inner == 2))
        & (slot_token % HALF == key_token % HALF)
        & (key_token // HALF <= slot_token // HALF)
    )
    stats = stat[...]
    top_row = jnp.max(stats, axis=0, keepdims=True)
    factors = jnp.exp(stats - top_row)
    totals = pltpu.roll(stats, HD - HALF, 1) + pltpu.roll(stats, HD - 2 * HALF, 1)
    turn[...] = jnp.zeros((HD, HD), f32)
    turn[0:PEERS, :] = factors
    turn[PEERS : PEERS + 1, :] = jnp.sum(factors * totals, axis=0, keepdims=True)
    turn[PEERS + 1 : PEERS + 2, :] = top_row
    turned = turn[...].T[0:HALF, :]
    total = turned[:, PEERS : PEERS + 1]
    top_cache = turned[:, PEERS + 1 : PEERS + 2]
    summed = jnp.zeros((HALF, HD), f32)
    for i in range(PEERS):
        summed = summed + turned[:, i : i + 1] * part_ref[i, 0:HALF, :].astype(f32)
    top_draft = jnp.max(jnp.where(visible, scores, FLOOR), axis=1, keepdims=True)
    top = jnp.maximum(top_cache, top_draft)
    weights = jnp.where(visible, jnp.exp(scores - top), 0.0)
    scale = jnp.exp(top_cache - top)
    total = scale * total + jnp.sum(weights, axis=1, keepdims=True)
    summed = scale * summed + nn_dot(pltpu.roll(weights, 1, 1).astype(bf16), drafts)
    attn = (summed / total).astype(bf16)
    for i in range(PEERS):
        out_ref[i] = attn


def project_kernel(token_ref, own_ref, oth_ref, w_ref, stream_ref, out_ref, by_token):
    tp = lax.axis_index("tp")
    acc = jnp.zeros((TOKS, COLS), f32)
    for i in range(HEADS // 2):
        lhs = jnp.concatenate(
            [
                jnp.concatenate([own_ref[2 * i], own_ref[2 * i + 1]], axis=1),
                jnp.concatenate([oth_ref[2 * i], oth_ref[2 * i + 1]], axis=1),
            ],
            axis=0,
        )
        acc = acc + nn_dot(lhs, w_ref[2 * i * HD : (2 * i + 2) * HD, :])
    place = (row_ids((TOKS, HD)) == token_ref[0:1, :]).astype(bf16)[:, :TOKS]
    high = acc.astype(bf16)
    rest = acc - high.astype(f32)
    middle = rest.astype(bf16)
    low = (rest - middle.astype(f32)).astype(bf16)
    split = nn_dot(place, jnp.concatenate([high, middle, low], axis=1))
    by_token[...] = split[:, :COLS] + (split[:, COLS : 2 * COLS] + split[:, 2 * COLS :])
    mine = pl.ds(pl.multiple_of(tp * 16, 16), 16)
    by_token[mine, :] = by_token[mine, :] + stream_ref[...].astype(f32)
    for y in range(NY):
        rows = by_token[16 * y : 16 * y + 16, :].astype(bf16)
        for z in range(NZ):
            out_ref[z * NY + y] = rows


def spread_kernel(in_ref, gain_ref, out_ref, mid_ref, whole):
    mine = lax.axis_index("kvp") // NC
    x = lax.rem(mine, NX)
    for z in range(NZ):
        parts = [in_ref[z * NY + y].astype(f32) for y in range(NY)]
        middle = (parts[0] + parts[1]) + (parts[2] + parts[3])
        whole[z] = middle
        scaled = (middle * gain_ref[pl.ds(z * NX + x, 1), :]).astype(bf16)
        for i in range(NX * NY):
            out_ref[i, z * 16 : (z + 1) * 16, :] = scaled
    mid_ref[...] = whole[mine // NX]


def token_rows(src_ref, i):
    z, x = i // NX, i % NX
    return jnp.concatenate(
        [src_ref[x * NY + y, z * 16 : (z + 1) * 16, :] for y in range(NY)], axis=0
    )


def gate_kernel(rows_ref, gain_ref, gu_ref, gu2_ref, sums_ref):
    core = lax.rem(lax.axis_index("kvp"), 2)
    sums = [jnp.zeros((TOKS, 2 * HIDDEN), f32) for _ in range(2)]
    squares = jnp.zeros((TOKS, COLS), f32)
    inverse = 1.0 / gain_ref[...]
    for i in range(PEERS):
        rows = token_rows(rows_ref, i)
        middle = rows.astype(f32) * inverse[i : i + 1, :]
        squares = squares + middle * middle
        cols = pl.ds(pl.multiple_of((2 * i + core) * COLS, COLS), COLS)
        for j, ref in enumerate((gu_ref, gu2_ref)):
            both = jnp.concatenate([ref[0, :, cols], ref[1, :, cols]], axis=0)
            sums[j] = sums[j] + nt_dot(rows, both)
    for j in range(2):
        sums_ref[j, :, : 2 * HIDDEN] = sums[j]
    sums_ref[2] = jnp.broadcast_to(jnp.sum(squares, axis=1, keepdims=True), (TOKS, COLS))


def down_kernel(own_ref, oth_ref, down_ref, down2_ref, out_ref):
    core = lax.rem(lax.axis_index("kvp"), 2)
    squares = own_ref[2][:, 0:1] + oth_ref[2][:, 0:1]
    rscale = lax.rsqrt(squares / D + EPS)
    hidden = []
    for j in range(2):
        total = (own_ref[j] + oth_ref[1 - j]) * rscale
        gate, up = total[:, :HIDDEN], total[:, HIDDEN : 2 * HIDDEN]
        hidden.append((gate / (1.0 + jnp.exp(-gate)) * up).astype(bf16))
    for i in range(PEERS):
        z, x = i // NX, i % NX
        cols = pl.ds(pl.multiple_of((2 * i + core) * COLS, COLS), COLS)
        part = nn_dot(hidden[0], down_ref[:, cols]) + nn_dot(hidden[1], down2_ref[:, cols])
        part = part.astype(bf16)
        for y in range(NY):
            line = jnp.where(core == 0, x, y)
            rest = (x + y - line) * NZ + z
            out_ref[line, pl.ds(pl.multiple_of(rest * 16, 16), 16), :] = part[
                16 * y : 16 * y + 16
            ]


def finish_kernel(parts_ref, middle_ref, out_ref):
    total = middle_ref[...]
    for i in range(4 * NZ):
        total = total + parts_ref[i].astype(f32)
    out_ref[...] = total.astype(bf16)


VMEM = pl.BlockSpec(memory_space=pltpu.VMEM)
SMEM = pl.BlockSpec(memory_space=pltpu.SMEM)
HBM = pl.BlockSpec(memory_space=pltpu.HBM)
COST = pl.CostEstimate(flops=10**9, bytes_accessed=4 * 10**7, transcendentals=0)
PARAMS = pltpu.CompilerParams(vmem_limit_bytes=VMEM_LIMIT)


def call(kernel, name, in_specs, out_shape, out_specs, scratch=(), cost=COST):
    return pl.pallas_call(
        kernel,
        name=name,
        in_specs=in_specs,
        out_shape=out_shape,
        out_specs=out_specs,
        scratch_shapes=list(scratch),
        compiler_params=PARAMS,
        cost_estimate=cost,
    )


def in_hbm(array):
    return pltpu.with_memory_space_constraint(array, pltpu.HBM)


def on_device(
    query,
    draft_kv,
    key_cache,
    value_cache,
    prompt_of,
    prefix_len,
    out_weight,
    stream,
    norm_gain,
    gate_up,
    down_weight,
):
    shape = jax.ShapeDtypeStruct
    cache = shape((PROMPTS // 2, SHARD, 2 * HD), bf16)
    key_pair, value_pair = swap_cores(key_cache), swap_cores(value_cache)
    draft_pair = swap_cores(draft_kv)
    block, keys, values, extra, order = call(
        prepare_kernel,
        "prepare",
        [HBM] * 7,
        [
            shape((PEERS, HEADS, HD), bf16),
            cache,
            cache,
            shape((2, 8, HD), f32),
            shape((TOKS + PROMPTS,), jnp.int32),
        ],
        [VMEM, VMEM, VMEM, VMEM, SMEM],
        [
            pltpu.VMEM((HEADS, HD), f32),
            pltpu.SMEM((PROMPTS,), jnp.int32),
            pltpu.SMEM((HALF,), jnp.int32),
            pltpu.SMEM((PROMPTS,), jnp.int32),
            pltpu.VMEM((1, HEADS * HD), bf16),
            pltpu.VMEM((1, 2, 2 * HD), bf16),
            pltpu.VMEM((COLS,), bf16),
            pltpu.SemaphoreType.DMA((7,)),
        ],
        None,
    )(
        in_hbm(prompt_of),
        in_hbm(prefix_len),
        in_hbm(query),
        in_hbm(draft_kv),
        in_hbm(norm_gain),
        in_hbm(key_cache),
        in_hbm(value_cache),
    )
    block, draft_pair, key_pair, value_pair = lax.optimization_barrier(
        (block, draft_pair, key_pair, value_pair)
    )
    own = swap_plane(block)
    oth = swap_cores(own)
    oth, gate_up_sent = lax.optimization_barrier((oth, gate_up))
    gate_up_pair = swap_cores(gate_up_sent)
    part, queries, slot_token, row_token = call(
        attention_kernel,
        "attention",
        [SMEM] + [VMEM] * 8,
        [
            shape((HEADS, ROWS_OUT, HD), bf16),
            shape((HALF, HEADS, HD), bf16),
            shape((HALF, HD), jnp.int32),
            shape((8, HD), jnp.int32),
        ],
        [VMEM] * 4,
        [pltpu.VMEM((TOKS, HEADS, HD), bf16), pltpu.VMEM((8, HD), f32)],
    )(
        order,
        own,
        oth,
        keys,
        values,
        key_pair,
        value_pair,
        extra,
        draft_pair,
    )
    attn, gains = call(
        combine_kernel,
        "combine",
        [VMEM, VMEM, VMEM],
        [shape((PEERS, HALF, HD), bf16), shape((PEERS, COLS), f32)],
        [VMEM, VMEM],
        [pltpu.VMEM((PEERS, HD), f32), pltpu.VMEM((HD, HD), f32)],
    )(swap_plane(part), queries, slot_token)
    attn_own = swap_plane(attn)
    attn_oth = swap_cores(attn_own)
    attn_oth, down_sent = lax.optimization_barrier((attn_oth, down_weight))
    down_pair = swap_cores(down_sent)
    partial = call(
        project_kernel,
        "project",
        [VMEM] * 5,
        shape((NZ * NY, 16, COLS), bf16),
        VMEM,
        [pltpu.VMEM((TOKS, COLS), f32)],
    )(row_token, attn_own, attn_oth, out_weight, stream)
    partial = lax.all_to_all(partial, ("kvp", "tp"), 0, 0, axis_index_groups=G_YZ, tiled=True)
    msg, middle = call(
        spread_kernel,
        "spread",
        [VMEM, VMEM],
        [shape((NX * NY, NZ * 16, COLS), bf16), shape((16, COLS), f32)],
        [VMEM, VMEM],
        [pltpu.VMEM((NZ, 16, COLS), f32)],
    )(partial, gains)
    normed = swap_face(msg)
    sums = call(
        gate_kernel,
        "gate",
        [VMEM] * 4,
        shape((3, TOKS, COLS), f32),
        VMEM,
    )(normed, gains, gate_up, gate_up_pair)
    partial = call(
        down_kernel,
        "down",
        [VMEM] * 4,
        shape((4, 4 * NZ * 16, COLS), bf16),
        VMEM,
    )(sums, swap_cores(sums), down_weight, down_pair)
    summed = lax.all_to_all(partial, ("kvp", "tp"), 0, 0, axis_index_groups=G_LINE, tiled=True)
    summed = jnp.sum(summed.astype(f32), axis=0).astype(bf16).reshape(4 * NZ, 16, COLS)
    summed = lax.all_to_all(summed, ("kvp", "tp"), 0, 0, axis_index_groups=G_REST, tiled=True)
    return call(finish_kernel, "finish", [VMEM, VMEM], shape((16, COLS), bf16), VMEM)(
        summed, middle
    )


def solution(mesh):
    in_specs = (
        P("kvp", "tp"),
        P("kvp", None, "tp"),
        P(None, "kvp", "tp"),
        P(None, "kvp", "tp"),
        P(),
        P(),
        P("tp", "kvp"),
        P("tp", "kvp"),
        P("kvp"),
        P(None, ("kvp", "tp"), None),
        P(("kvp", "tp"), None),
    )
    out_specs = P("tp", "kvp")
    return jax.shard_map(
        on_device, mesh=mesh, in_specs=in_specs, out_specs=out_specs, check_vma=False
    )
```
